32 devices in a mesh: grp: 4 (over y, core), pair: 8 (over z, x).
Axes of the slice: x: 2, y: 2, z: 4, core: 2. Of those that a mesh axis runs over, the one named last changes fastest.
Arguments:
- amplitudes: bfloat16 [512, 10368], P('pair'), may hold values from -6 to 6
- integrals: bfloat16 [10368, 10368], P('pair', 'grp'), may hold values from -0.0625 to 0.0625
- hole_ints: bfloat16 [512, 512], replicated, may hold values from -0.25 to 0.25
- driver: bfloat16 [512, 10368], P('pair', 'grp'), may hold values from -6 to 6
- e_occ: float32 [128], replicated, may hold values from -1.2 to -0.2
- e_virt: float32 [288], replicated, may hold values from 0.3 to 1.5
- occ_pairs: int32 [2, 512], P(None, 'pair'), may hold values from 0 to 127
- virt_pairs: int32 [2, 10368], P(None, 'grp'), may hold values from 0 to 287
Outputs:
- amp_next: float32 [512, 10368], P('pair')
The draws below stay inside these ranges and needn't reach their ends.
All inputs are finite; a program needn't handle non-finite values.
Results may differ from the reference program's by a relative error of at most 0.0003.
Values may be sent and summed in bfloat16 or wider, within the bound.
No kernel may reach another device: no remote copies, remote signals or barrier semaphores. Data moves between devices by JAX's collectives and lax.ppermute only.
A program may use at most 128 MiB of HBM per device.

```python
import jax
import jax.numpy as jnp

OCC = 128
NV = 288
VP = 10368
PAIRS = 512


def with_ends(drawn, stream_key, least, largest):
    longest = drawn.shape.index(max(drawn.shape))
    spots = []
    for shift in (0, 1):
        where = [jax.random.randint(jax.random.fold_in(stream_key, axis), (), 0, length) for axis, length in enumerate(drawn.shape)]
        where[longest] = (where[longest] + shift) % drawn.shape[longest]
        spots.append(tuple(where))
    return drawn.at[spots[0]].set(least).at[spots[1]].set(largest)


def levels(stream_key, dims, shards, smallest, high):
    loudness = 1.0
    for axis_at, parts in shards:
        steps = jax.random.uniform(jax.random.fold_in(jax.random.fold_in(stream_key, 6), axis_at), (parts,), jnp.float32, smallest / len(shards), high / len(shards))
        loudness = loudness * jnp.repeat(jnp.exp(steps), dims[axis_at] // parts).reshape((-1,) + (1,) * (len(dims) - 1 - axis_at))
    return loudness


def noise(stream_key, extent, scale, most, shards=(), kind=jnp.bfloat16):
    array = scale * jax.random.normal(stream_key, extent, jnp.float32)
    if shards:
        array = array * levels(stream_key, extent, shards, -0.22, 0.18)
    return jnp.clip(array, -most, most).astype(kind)


def setup_inputs(seed: int = 0) -> dict:
    key_of = jax.random.split(jax.random.key(seed), 9)
    return {
        "amplitudes": noise(key_of[0], (PAIRS, VP), 1.0, 6.0, ((0, 8),)),
        "integrals": noise(key_of[1], (VP, VP), VP ** -0.5, 0.0625, ((0, 8), (1, 4))),
        "hole_ints": noise(key_of[2], (PAIRS, PAIRS), PAIRS ** -0.5, 0.25),
        "driver": noise(key_of[3], (PAIRS, VP), 1.0, 6.0, ((0, 8), (1, 4))),
        "e_occ": jnp.clip(jax.random.uniform(key_of[4], (OCC,), jnp.float32, -1.2, -0.2), -1.2, -0.2),
        "e_virt": jnp.clip(jax.random.uniform(key_of[5], (NV,), jnp.float32, 0.3, 1.5), 0.3, 1.5),
        "occ_pairs": with_ends(jax.random.randint(key_of[6], (2, PAIRS), 0, OCC), jax.random.fold_in(key_of[6], 1), 0, OCC - 1).astype(jnp.int32),
        "virt_pairs": with_ends(jax.random.randint(key_of[7], (2, VP), 0, NV), jax.random.fold_in(key_of[7], 1), 0, NV - 1).astype(jnp.int32),
    }


def reference(amplitudes, integrals, hole_ints, driver, e_occ, e_virt, occ_pairs, virt_pairs):
    particle = jnp.dot(amplitudes, integrals, preferred_element_type=jnp.float32)
    hole_term = jnp.dot(hole_ints, amplitudes, preferred_element_type=jnp.float32)
    ladder = particle + hole_term
    hole_energy = e_occ[occ_pairs[0]] + e_occ[occ_pairs[1]]
    pair_energy = e_virt[virt_pairs[0]] + e_virt[virt_pairs[1]]
    energy_gap = pair_energy[None, :] - hole_energy[:, None]
    return (driver.astype(jnp.float32) + ladder) / energy_gap
```

```python
import functools
import math

import jax
import jax.numpy as jnp
from jax import lax
from jax.experimental import pallas as pl
from jax.experimental.pallas import tpu as pltpu
from jax.sharding import PartitionSpec as P

TOP = 32752.0
STEP = 0.0625
LANES = 128
VMEM_LIMIT = 48 * 1024 * 1024
CUT_LIMIT = 8 * 1024 * 1024
SMALL = pl.CostEstimate(flops=1024, bytes_accessed=1024, transcendentals=0)


def lookup(labels, energies):
    table = lax.broadcasted_iota(jnp.int32, labels.shape + energies.shape, labels.ndim)
    picked = jnp.where(labels[..., None] == table, energies, jnp.float32(0.0))
    return jnp.sum(picked, axis=-1)


def layout(cols):
    width = cols // LANES * LANES + LANES
    tiles = width // LANES
    segments = next(n for n in (3, 2, 1) if tiles % n == 0)
    return width, segments


def columns(rows, size, start):
    return lax.broadcasted_iota(jnp.int32, (rows, size), 1) + start


def encode(x):
    most = jnp.max(jnp.abs(x), axis=1, keepdims=True)
    code = jnp.ceil(jnp.log2(jnp.maximum(most, 1e-30)) * (1.0 / STEP))
    whole = jnp.round(x * (jnp.exp2(code * -STEP) * TOP))
    return whole.astype(jnp.int32), code


def with_codes(whole, codes, cols, start):
    at = columns(whole.shape[0], whole.shape[1], start)
    for n, code in enumerate(codes):
        whole = jnp.where(at == cols + n, code.astype(jnp.int32), whole)
    return whole


def decode(coded, codes, n, cols, start):
    x = coded.astype(jnp.float32) * (jnp.exp2(codes[n] * STEP) * (1.0 / TOP))
    if start + x.shape[1] > cols:
        x = jnp.where(columns(x.shape[0], x.shape[1], start) < cols, x, 0.0)
    return x


def codes_of(coded_ref, at, cols, segments):
    tail = coded_ref[at, cols // LANES * LANES :].astype(jnp.float32)
    first = cols % LANES
    return [tail[:, first + n : first + n + 1] for n in range(segments)]


def in_hbm(x):
    return pltpu.with_memory_space_constraint(x, pltpu.HBM)


def params(*dims, limit=VMEM_LIMIT):
    return pltpu.CompilerParams(
        dimension_semantics=dims or None, vmem_limit_bytes=limit
    )


def turns(count):
    return [*range(count // 2, count), *range(count // 2 - 1, -1, -1)]


def cut_kernel(where, a_ref, *refs):
    outs, slots = refs[:-1], refs[-1]
    count, _, depth = slots.shape
    for n in range(2 * count):
        k = where[0] ^ n

        @pl.when(k % 2 == where[2])
        def _():
            slots[k // 2] = a_ref[:, n * depth : (n + 1) * depth]

    for j, turn in enumerate(turns(count)):
        outs[j][...] = slots[turn]


def cut(amplitudes, pair, part, core, pairs, depth):
    rows, total = amplitudes.shape
    high, count = rows // 2, pairs // 2
    return pl.pallas_call(
        cut_kernel,
        grid_spec=pltpu.PrefetchScalarGridSpec(
            num_scalar_prefetch=1,
            grid=(1,),
            in_specs=[pl.BlockSpec((high, total), lambda i, where: (where[1], 0))],
            out_specs=[pl.BlockSpec((high, depth), lambda i, where: (0, 0))] * count,
            scratch_shapes=[pltpu.VMEM((count, high, depth), jnp.bfloat16)],
        ),
        out_shape=[jax.ShapeDtypeStruct((high, depth), jnp.bfloat16)] * count,
        compiler_params=params("arbitrary", limit=CUT_LIMIT),
        cost_estimate=SMALL,
        name="cut_blocks",
    )(jnp.stack([pair, part, core]), in_hbm(amplitudes))


def pack_kernel(count, *refs):
    for n in range(count):
        refs[-1][n] = refs[n][...]


def pack(blocks, others):
    shape = (len(blocks),) + blocks[0].shape
    return pl.pallas_call(
        functools.partial(pack_kernel, len(blocks)),
        in_specs=[pl.BlockSpec(memory_space=pltpu.VMEM)] * len(blocks)
        + [pl.BlockSpec(memory_space=pl.ANY)] * len(others),
        out_shape=jax.ShapeDtypeStruct(shape, jnp.bfloat16),
        compiler_params=params(limit=CUT_LIMIT),
        cost_estimate=SMALL,
        name="pack_blocks",
    )(*blocks, *others)


def product_kernel(order, parts, cols, segments, where, *refs):
    a_refs, (h_ref, v_ref, o_ref), outs = refs[:parts], refs[parts : parts + 3], refs[parts + 3 : -4]
    left, left_rest, right_rest, codes = refs[-4:]
    part, depth = a_refs[0].shape[1] // parts, a_refs[0].shape[2]
    rows = o_ref.shape[0]
    main, second = split_depth(depth)
    step = pl.program_id(0)
    tile = v_ref.shape[1]
    high = outs[0].shape[0]

    @pl.when(step == 0)
    def _():
        left_rest[...] = jnp.zeros_like(left_rest)
        right_rest[...] = jnp.zeros_like(right_rest)
        count = a_refs[0].shape[0]
        spot = {entry: n for n, entry in enumerate(order)}
        for s, ref in enumerate(a_refs):
            swapped = where[1] ^ s
            for j, turn in enumerate(turns(count)):
                for q in range(parts):
                    even, odd = spot[q, 2 * turn], spot[q, 2 * turn + 1]
                    at = jnp.where(swapped == 0, even, odd) * part
                    at = pl.ds(pl.multiple_of(at, part), part)
                    block = ref.at[j, q * part : (q + 1) * part]
                    left[at, :] = block[:, :main]
                    left_rest[at, : depth - main] = block[:, main:]
                    source = where[0] ^ (2 * turn + swapped)
                    left_rest[at, second : second + rows] = h_ref[source, where[2 + q]]

    right_rest[: depth - main, :] = v_ref[main:, :]
    right_rest[second : second + rows, :] = o_ref[...]
    acc = jnp.dot(left[...], v_ref[:main, :], preferred_element_type=jnp.float32)
    acc = acc + jnp.dot(left_rest[...], right_rest[...], preferred_element_type=jnp.float32)
    acc = jnp.where(columns(acc.shape[0], tile, step * tile) < cols, acc, 0.0)
    given = parts * high
    for j in range(parts):
        outs[parts + j][...] = acc[given + j * high : given + (j + 1) * high]
    whole, code = encode(acc[:given])
    at = lax.broadcasted_iota(jnp.int32, codes.shape, 1)
    codes[...] = jnp.where(at == step, code, codes[...])

    @pl.when(step < segments - 1)
    def _():
        for j in range(parts):
            outs[j][...] = whole[j * high : (j + 1) * high].astype(jnp.int16)

    @pl.when(step == segments - 1)
    def _():
        kept = [codes[:, n : n + 1] for n in range(segments)]
        done = with_codes(whole, kept, cols, (segments - 1) * tile)
        for j in range(parts):
            outs[j][...] = done[j * high : (j + 1) * high].astype(jnp.int16)


def split_depth(depth):
    main = depth // LANES * LANES
    return main, -(-(depth - main) // 16) * 16


def product(order, where, sources, holes, integrals, own_cols):
    parts = len(sources)
    _, high_block, depth = sources[0].shape
    part = high_block // parts
    cols = integrals.shape[1]
    rows = own_cols.shape[0]
    width, segments = layout(cols)
    tile = width // segments
    total = len(order) * part
    high = total // (2 * parts)
    main, second = split_depth(depth)
    rest = -(-(second + rows) // LANES) * LANES
    whole = lambda x: pl.BlockSpec(x.shape, lambda i, where: (0,) * x.ndim)
    out = pl.BlockSpec((high, tile), lambda i, where: (0, i))
    return pl.pallas_call(
        functools.partial(product_kernel, order, parts, cols, segments),
        grid_spec=pltpu.PrefetchScalarGridSpec(
            num_scalar_prefetch=1,
            grid=(segments,),
            in_specs=[whole(x) for x in sources]
            + [
                whole(holes),
                pl.BlockSpec((depth, tile), lambda i, where: (0, i)),
                pl.BlockSpec((rows, tile), lambda i, where: (0, i)),
            ],
            out_specs=[out] * (2 * parts),
            scratch_shapes=[
                pltpu.VMEM((total, main), jnp.bfloat16),
                pltpu.VMEM((total, rest), jnp.bfloat16),
                pltpu.VMEM((rest, tile), jnp.bfloat16),
                pltpu.VMEM((total // 2, LANES), jnp.float32),
            ],
        ),
        out_shape=[jax.ShapeDtypeStruct((high, width), jnp.int16)] * parts
        + [jax.ShapeDtypeStruct((high, width), jnp.float32)] * parts,
        compiler_params=params("arbitrary"),
        cost_estimate=SMALL,
        name="partial_products",
    )(where, *sources, in_hbm(holes), integrals, in_hbm(own_cols))


def add_kernel(cols, segments, inputs, inner, *refs):
    keeps, coded, (give_ref, next_ref) = refs[:inputs], refs[inputs : 2 * inputs], refs[2 * inputs :]
    high, width = next_ref.shape
    half = high // (inputs * inner)
    tile = width // segments
    chunk = min(16, half)

    for index in range(inputs):
        keep_ref, coded_ref = keeps[index], coded[index]

        def total(at, n, codes):
            span = slice(n * tile, (n + 1) * tile)
            return keep_ref[at, span] + decode(coded_ref[at, span], codes, n, cols, n * tile)

        for group in range(inner):
            top, target = 2 * half * group, half * (inner * index + group)

            @pl.loop(0, half // chunk)
            def _(i):
                out = pl.ds(pl.multiple_of(target + i * chunk, chunk), chunk)
                at = pl.ds(pl.multiple_of(top + i * chunk, chunk), chunk)
                codes = codes_of(coded_ref, at, cols, segments)
                made = []
                for n in range(segments):
                    whole, code = encode(total(at, n, codes))
                    made.append(code)
                    if n == segments - 1:
                        whole = with_codes(whole, made, cols, n * tile)
                    give_ref[out, n * tile : (n + 1) * tile] = whole.astype(jnp.int16)

            @pl.loop(0, half // chunk)
            def _(i):
                out = pl.ds(pl.multiple_of(target + i * chunk, chunk), chunk)
                at = pl.ds(pl.multiple_of(top + half + i * chunk, chunk), chunk)
                codes = codes_of(coded_ref, at, cols, segments)
                for n in range(segments):
                    next_ref[out, n * tile : (n + 1) * tile] = total(at, n, codes)


def add(keeps, coded, inner, cols):
    high, width = keeps[0].shape
    out = (len(keeps) * high // 2, width)
    return pl.pallas_call(
        functools.partial(add_kernel, cols, layout(cols)[1], len(keeps), inner),
        out_shape=(
            jax.ShapeDtypeStruct(out, jnp.int16),
            jax.ShapeDtypeStruct(out, jnp.float32),
        ),
        compiler_params=params(),
        cost_estimate=SMALL,
        name="add_partial_sums",
    )(*keeps, *coded)


def update_kernel(cols, segments, inputs, where, *refs):
    keeps, coded, (d_ref, v_ref, o_ref, out_ref) = refs[:inputs], refs[inputs : 2 * inputs], refs[2 * inputs :]
    width = out_ref.shape[1]
    tile = width // segments
    part = out_ref.shape[0] // 2
    for j in range(2):
        keep_ref, coded_ref = keeps[j % inputs], coded[j % inputs]
        at = pl.ds((j // inputs) * part, part)
        here = pl.ds(pl.multiple_of(where[j] * part, part), part)
        mine = pl.ds(pl.multiple_of((where[j] % 2) * part, part), part)
        codes = codes_of(coded_ref, at, cols, segments)
        made = []
        for n in range(segments):
            start, stop = n * tile, (n + 1) * tile
            ladder = keep_ref[at, start:stop]
            ladder = ladder + decode(coded_ref[at, start:stop], codes, n, cols, start)
            driver = d_ref[mine, start : min(stop, cols)].astype(jnp.float32)
            if stop > cols:
                driver = jnp.concatenate(
                    [driver, jnp.zeros((part, stop - cols), jnp.float32)], axis=1
                )
            gap = v_ref[:, start:stop] - o_ref[here, 0:1]
            whole, code = encode((driver + ladder) / gap)
            made.append(code)
            if n == segments - 1:
                whole = with_codes(whole, made, cols, start)
            out_ref[j * part : (j + 1) * part, start:stop] = whole.astype(jnp.int16)


def updated(keeps, coded, driver, pair_energy, hole_energy, where, cols):
    high, width = keeps[0].shape
    high *= len(keeps)
    whole = lambda x: pl.BlockSpec(x.shape, lambda i, where: (0,) * x.ndim)
    return pl.pallas_call(
        functools.partial(update_kernel, cols, layout(cols)[1], len(keeps)),
        grid_spec=pltpu.PrefetchScalarGridSpec(
            num_scalar_prefetch=1,
            grid=(1,),
            in_specs=[whole(x) for x in (*keeps, *coded)]
            + [pl.BlockSpec((high, cols), lambda i, where: (where[0] // 2, 0))]
            + [whole(pair_energy), whole(hole_energy)],
            out_specs=pl.BlockSpec((high, width), lambda i, where: (0, 0)),
        ),
        out_shape=jax.ShapeDtypeStruct((high, width), jnp.int16),
        compiler_params=params("arbitrary"),
        cost_estimate=SMALL,
        name="update_amplitudes",
    )(where, *keeps, *coded, driver, pair_energy, hole_energy)


def place_kernel(cols, segments, groups, where, *refs):
    out_ref, slots = refs[-2:]
    rows = out_ref.shape[0]
    part = rows // 4
    width = refs[0].shape[1]
    tile = width // segments
    for index in range(2 * groups):
        rel, half = index // 2, index % 2
        ref = refs[index]
        group = where[0] ^ rel
        shift = (group * cols) % LANES
        for j in range(2):
            at = pl.ds(j * part, part)
            codes = codes_of(ref, at, cols, segments)
            pieces = [
                decode(ref[at, n * tile : (n + 1) * tile], codes, n, cols, n * tile)
                for n in range(segments)
            ]
            pieces += [jnp.zeros((part, slots.shape[2] - width), jnp.float32)] * (
                slots.shape[2] > width
            )
            x = pltpu.roll(jnp.concatenate(pieces, axis=1), shift, 1)
            quarter = 2 * ((group // 2) % 2 ^ half) + j
            slots[group, pl.ds(pl.multiple_of(quarter * part, part), part), :] = x
    lane = lax.broadcasted_iota(jnp.int32, (rows, LANES), 1)
    for group in range(groups):
        start = group * cols
        base, shift = start // LANES * LANES, start % LANES
        full = (shift + cols) // LANES * LANES
        if group == groups - 1:
            full = shift + cols
        first = 0
        if shift:
            before = (group - 1) * cols % LANES + cols
            before = before // LANES * LANES
            tail = slots[group - 1, :, before : before + LANES]
            out_ref[:, base : base + LANES] = jnp.where(
                lane < shift, tail, slots[group, :, 0:LANES]
            )
            first = LANES
        out_ref[:, base + first : base + full] = slots[group, :, first:full]


def place(blocks, grp, rows, cols, groups):
    width, segments = layout(cols)
    unit = math.gcd(cols, LANES)
    room = width + LANES * (cols % LANES > unit)
    whole = lambda shape: pl.BlockSpec(shape, lambda i, where: (0,) * len(shape))
    out = (rows, groups * cols)
    return pl.pallas_call(
        functools.partial(place_kernel, cols, segments, groups),
        grid_spec=pltpu.PrefetchScalarGridSpec(
            num_scalar_prefetch=1,
            grid=(1,),
            in_specs=[whole(x.shape) for x in blocks],
            out_specs=whole(out),
            scratch_shapes=[pltpu.VMEM((groups, rows, room), jnp.float32)],
        ),
        out_shape=jax.ShapeDtypeStruct(out, jnp.float32),
        compiler_params=params("arbitrary"),
        name="place_columns",
    )(grp, *blocks)


def spans_of(cols, chip):
    first = chip * 2 * cols % LANES
    second = first + cols
    return first, second // LANES, second % LANES, -(-(second + cols) // LANES)


def half_kernel(cols, segments, late, where, *refs):
    coded, refs = refs[:4], refs[4:]
    if late:
        seam_in, _, out_ref, slots, strips, sems = refs
    else:
        out_ref, seam_ref, slots, strips, sems = refs
    high = coded[0].shape[0]
    part = high // 2
    width = coded[0].shape[1]
    tile = width // segments
    for rel, ref in enumerate(coded):
        group = where[0] ^ rel
        for j in range(2):
            at = pl.ds(j * part, part)
            codes = codes_of(ref, at, cols, segments)
            pieces = [
                decode(ref[at, n * tile : (n + 1) * tile], codes, n, cols, n * tile)
                for n in range(segments)
            ]
            x = pltpu.roll(jnp.concatenate(pieces, axis=1), (group * cols) % LANES, 1)
            slots[group, j * part : (j + 1) * part, :] = x
    lane = lax.broadcasted_iota(jnp.int32, (high, LANES), 1)
    stores = []
    for chip in range(2):
        _, turn, shift, tiles = spans_of(cols, chip)
        one, two = slots.at[2 * chip], slots.at[2 * chip + 1]
        strip = strips.at[chip]
        strip[:, : turn * LANES] = one[:, : turn * LANES]
        seam = turn * LANES
        strip[:, seam : seam + LANES] = jnp.where(
            lane < shift, one[:, seam : seam + LANES], two[:, :LANES]
        )
        strip[:, seam + LANES : tiles * LANES] = two[:, LANES : tiles * LANES - seam]
        top = (chip ^ late) * high
        shared = slice(0, LANES) if chip else slice((tiles - 1) * LANES, tiles * LANES)
        if late:
            strip[:, shared] = strip[:, shared] + seam_in[top : top + high, :]
            start, stop = 0, tiles * LANES
        else:
            seam_ref[top : top + high, :] = strip[:, shared]
            start, stop = (LANES, tiles * LANES) if chip else (0, (tiles - 1) * LANES)
        base = chip * 2 * cols // LANES * LANES
        store = pltpu.make_async_copy(
            strip.at[:, start:stop],
            out_ref.at[top : top + high, base + start : base + stop],
            sems.at[chip],
        )
        store.start()
        stores.append(store)
    for store in stores:
        store.wait()


def place_half(blocks, grp, rows, cols, so_far=None):
    width, segments = layout(cols)
    high = rows // 2
    tiles = max(spans_of(cols, chip)[3] for chip in range(2))
    whole = lambda x: pl.BlockSpec(x.shape, lambda i, where: (0,) * x.ndim)
    anywhere = pl.BlockSpec(memory_space=pl.ANY)
    out = jax.ShapeDtypeStruct((rows, 4 * cols), jnp.float32)
    seam = jax.ShapeDtypeStruct((rows, LANES), jnp.float32)
    late = so_far is not None
    return pl.pallas_call(
        functools.partial(half_kernel, cols, segments, late),
        grid_spec=pltpu.PrefetchScalarGridSpec(
            num_scalar_prefetch=1,
            grid=(1,),
            in_specs=[whole(x) for x in blocks] + [whole(seam), anywhere] * late,
            out_specs=anywhere if late else (anywhere, whole(seam)),
            scratch_shapes=[
                pltpu.VMEM((4, high, width), jnp.float32),
                pltpu.VMEM((2, high, tiles * LANES), jnp.float32),
                pltpu.SemaphoreType.DMA((2,)),
            ],
        ),
        out_shape=out if late else (out, seam),
        input_output_aliases={6: 0} if late else {},
        compiler_params=params("arbitrary"),
        name="place_late_half" if late else "place_early_half",
    )(grp, *blocks, *(so_far[::-1] if late else ()))


def shards(amplitudes, integrals, hole_ints, driver, e_occ, e_virt, occ_pairs, virt_pairs):
    groups, pairs = lax.axis_size("grp"), lax.axis_size("pair")
    grp, pair = lax.axis_index("grp"), lax.axis_index("pair")
    rows = amplitudes.shape[0]
    part = rows // 4
    depth, cols = integrals.shape
    width, _ = layout(cols)

    def swap(x, axis, flip):
        size = lax.axis_size(axis)
        return lax.ppermute(x, axis, [(i, i ^ flip) for i in range(size)])

    own_cols = lax.dynamic_slice_in_dim(amplitudes, grp * cols, cols, 1)
    holes = lax.dynamic_slice_in_dim(hole_ints, pair * rows, rows, 1)
    holes = holes.reshape(pairs, 4, part, rows)
    chip_half, core_at, count = (grp // 2) % 2, grp % 2, pairs // 2
    blocks = list(cut(amplitudes, pair, chip_half, core_at, pairs, depth))
    for j, turn in enumerate(turns(count)):
        moves = [
            (g * pairs + p, g * pairs + (p ^ (2 * turn + g % 2)))
            for g in range(groups)
            for p in range(pairs)
        ]
        blocks[j] = lax.ppermute(blocks[j], ("grp", "pair"), moves)
    own = pack(blocks, (own_cols, holes))
    core = swap(own, "grp", 1)
    chip = swap(own, "grp", 2)

    bits = [1 << n for n in range(pairs.bit_length() - 1)]
    x_first, z_first = bits, bits[1::-1] + bits[2:]
    x_then_far = bits[:1] + bits[2:] + bits[1:2]
    routes = ((z_first, x_then_far), (x_then_far, z_first))

    def listed(value, left):
        if not left:
            return [value]
        return listed(value | left[0], left[1:]) + listed(value, left[1:])

    def place_of(half):
        first = 2 * (chip_half ^ half)
        return jnp.stack([first, first + 1])

    def products(half, *sources):
        given = [(q, k) for q, r in enumerate(routes[half]) for k in listed(r[0], r[1:])]
        order = given + [(q, k ^ routes[half][q][0]) for q, k in given]
        where = jnp.concatenate([jnp.stack([pair, core_at]), place_of(half)])
        made = product(order, where, sources, holes, integrals, own_cols)
        return list(zip(made[:2], made[2:]))

    first = products(0, own, core)
    chip, _ = lax.optimization_barrier((chip, first[0][1]))
    both = swap(chip, "grp", 1)
    second = products(1, chip, both)

    state = [first, second]
    for n in range(len(bits)):
        for half in range(2):
            one, two = routes[half]
            steps = [one[n]] if len(state[half]) == 1 else [one[n], two[n]]
            got = [swap(give, "pair", bit) for (give, _), bit in zip(state[half], steps)]
            keeps = [keep for _, keep in state[half]]
            inner = 3 - len(keeps)
            if n == 0 and half == 0:
                after_first = got[0]
            if n == len(bits) - 1:
                state[half] = (keeps, got)
            elif inner == 2 or one[n + 1 :] == two[n + 1 :]:
                state[half] = [add(keeps, got, inner, cols)]
            else:
                state[half] = [add([k], [g], 1, cols) for k, g in zip(keeps, got)]
    (occ_pairs, virt_pairs), _ = lax.optimization_barrier(
        ((occ_pairs, virt_pairs), after_first)
    )
    occ_energy = lookup(occ_pairs, e_occ)
    virt_energy = lookup(virt_pairs, e_virt)
    hole_energy = jnp.broadcast_to((occ_energy[0] + occ_energy[1])[:, None], (rows, LANES))
    pair_energy = jnp.pad(
        (virt_energy[0] + virt_energy[1])[None, :],
        ((0, 0), (0, width - cols)),
        constant_values=8.0,
    )

    sent = []
    in_halves = groups == 4 and 2 * cols % LANES != 0
    for half in range(2):
        keeps, got = state[half]
        coded = updated(keeps, got, driver, pair_energy, hole_energy, place_of(half), cols)
        here = [coded] + [swap(coded, "grp", 2 * k) for k in range(1, groups // 2)]
        if half and in_halves:
            early = place_half(sent[0], grp[None], rows, cols)
        sent.append([x for own_x in here for x in (own_x, swap(own_x, "grp", 1))])

    if in_halves:
        return place_half(sent[1], grp[None], rows, cols, early)
    ordered = [sent[half][rel] for rel in range(groups) for half in range(2)]
    return place(ordered, grp[None], rows, cols, groups)


def solution(mesh):
    placed = (
        P("pair", None),
        P("pair", "grp"),
        P(),
        P("pair", "grp"),
        P(),
        P(),
        P(None, "pair"),
        P(None, "grp"),
    )
    return jax.shard_map(
        shards, mesh=mesh, in_specs=placed, out_specs=P("pair", None), check_vma=False
    )
```

```python
import functools
import math

import jax
import jax.numpy as jnp
from jax import lax
from jax.experimental import pallas as pl
from jax.experimental.pallas import tpu as pltpu
from jax.sharding import PartitionSpec as P

TOP = 32752.0
STEP = 0.0625
LANES = 128
VMEM_LIMIT = 48 * 1024 * 1024
CUT_LIMIT = 8 * 1024 * 1024
SMALL = pl.CostEstimate(flops=1024, bytes_accessed=1024, transcendentals=0)


def lookup(labels, energies):
    table = lax.broadcasted_iota(jnp.int32, labels.shape + energies.shape, labels.ndim)
    picked = jnp.where(labels[..., None] == table, energies, jnp.float32(0.0))
    return jnp.sum(picked, axis=-1)


def layout(cols):
    width = cols // LANES * LANES + LANES
    tiles = width // LANES
    segments = next(n for n in (3, 2, 1) if tiles % n == 0)
    return width, segments


def columns(rows, size, start):
    return lax.broadcasted_iota(jnp.int32, (rows, size), 1) + start


def encode(x):
    most = jnp.max(jnp.abs(x), axis=1, keepdims=True)
    code = jnp.ceil(jnp.log2(jnp.maximum(most, 1e-30)) * (1.0 / STEP))
    whole = jnp.round(x * (jnp.exp2(code * -STEP) * TOP))
    return whole.astype(jnp.int32), code


def with_codes(whole, codes, cols, start):
    at = columns(whole.shape[0], whole.shape[1], start)
    for n, code in enumerate(codes):
        whole = jnp.where(at == cols + n, code.astype(jnp.int32), whole)
    return whole


def decode(coded, codes, n, cols, start):
    x = coded.astype(jnp.float32) * (jnp.exp2(codes[n] * STEP) * (1.0 / TOP))
    if start + x.shape[1] > cols:
        x = jnp.where(columns(x.shape[0], x.shape[1], start) < cols, x, 0.0)
    return x


def codes_of(coded_ref, at, cols, segments):
    tail = coded_ref[at, cols // LANES * LANES :].astype(jnp.float32)
    first = cols % LANES
    return [tail[:, first + n : first + n + 1] for n in range(segments)]


def in_hbm(x):
    return pltpu.with_memory_space_constraint(x, pltpu.HBM)


def params(*dims, limit=VMEM_LIMIT):
    return pltpu.CompilerParams(
        dimension_semantics=dims or None, vmem_limit_bytes=limit
    )


def cut_kernel(where, a_ref, *refs):
    outs, slots = refs[:-1], refs[-1]
    count, _, depth = slots.shape
    for n in range(2 * count):
        k = where[0] ^ n

        @pl.when(k // count == where[2])
        def _():
            slots[k % count] = a_ref[:, n * depth : (n + 1) * depth]

    for j in range(count):
        outs[j][...] = slots[(j + 1) % count]


def cut(amplitudes, pair, part, core, pairs, depth):
    rows, total = amplitudes.shape
    high, count = rows // 2, pairs // 2
    return pl.pallas_call(
        cut_kernel,
        grid_spec=pltpu.PrefetchScalarGridSpec(
            num_scalar_prefetch=1,
            grid=(1,),
            in_specs=[pl.BlockSpec((high, total), lambda i, where: (where[1], 0))],
            out_specs=[pl.BlockSpec((high, depth), lambda i, where: (0, 0))] * count,
            scratch_shapes=[pltpu.VMEM((count, high, depth), jnp.bfloat16)],
        ),
        out_shape=[jax.ShapeDtypeStruct((high, depth), jnp.bfloat16)] * count,
        compiler_params=params("arbitrary", limit=CUT_LIMIT),
        cost_estimate=SMALL,
        name="cut_blocks",
    )(jnp.stack([pair, part, core]), in_hbm(amplitudes))


def pack_kernel(count, *refs):
    for n in range(count):
        refs[-1][n] = refs[n][...]


def pack(blocks, others):
    shape = (len(blocks),) + blocks[0].shape
    return pl.pallas_call(
        functools.partial(pack_kernel, len(blocks)),
        in_specs=[pl.BlockSpec(memory_space=pltpu.VMEM)] * len(blocks)
        + [pl.BlockSpec(memory_space=pl.ANY)] * len(others),
        out_shape=jax.ShapeDtypeStruct(shape, jnp.bfloat16),
        compiler_params=params(limit=CUT_LIMIT),
        cost_estimate=SMALL,
        name="pack_blocks",
    )(*blocks, *others)


def product_kernel(order, parts, cols, segments, where, *refs):
    a_refs, (h_ref, v_ref, o_ref), outs = refs[:parts], refs[parts : parts + 3], refs[parts + 3 : -4]
    left, left_rest, right_rest, codes = refs[-4:]
    part, depth = a_refs[0].shape[1] // parts, a_refs[0].shape[2]
    rows = o_ref.shape[0]
    main, second = split_depth(depth)
    step = pl.program_id(0)
    tile = v_ref.shape[1]
    high = outs[0].shape[0]

    @pl.when(step == 0)
    def _():
        left_rest[...] = jnp.zeros_like(left_rest)
        right_rest[...] = jnp.zeros_like(right_rest)
        count = a_refs[0].shape[0]
        spot = {entry: n for n, entry in enumerate(order)}
        for s, ref in enumerate(a_refs):
            swapped = where[1] ^ s
            for j in range(count):
                low = (j + 1) % count
                for q in range(parts):
                    near, far = spot[q, low], spot[q, low + count]
                    at = jnp.where(swapped == 0, near, far) * part
                    at = pl.ds(pl.multiple_of(at, part), part)
                    block = ref.at[j, q * part : (q + 1) * part]
                    left[at, :] = block[:, :main]
                    left_rest[at, : depth - main] = block[:, main:]
                    source = where[0] ^ (low + count * swapped)
                    left_rest[at, second : second + rows] = h_ref[source, where[2 + q]]

    right_rest[: depth - main, :] = v_ref[main:, :]
    right_rest[second : second + rows, :] = o_ref[...]
    acc = jnp.dot(left[...], v_ref[:main, :], preferred_element_type=jnp.float32)
    acc = acc + jnp.dot(left_rest[...], right_rest[...], preferred_element_type=jnp.float32)
    acc = jnp.where(columns(acc.shape[0], tile, step * tile) < cols, acc, 0.0)
    given = parts * high
    for j in range(parts):
        outs[parts + j][...] = acc[given + j * high : given + (j + 1) * high]
    whole, code = encode(acc[:given])
    at = lax.broadcasted_iota(jnp.int32, codes.shape, 1)
    codes[...] = jnp.where(at == step, code, codes[...])

    @pl.when(step < segments - 1)
    def _():
        for j in range(parts):
            outs[j][...] = whole[j * high : (j + 1) * high].astype(jnp.int16)

    @pl.when(step == segments - 1)
    def _():
        kept = [codes[:, n : n + 1] for n in range(segments)]
        done = with_codes(whole, kept, cols, (segments - 1) * tile)
        for j in range(parts):
            outs[j][...] = done[j * high : (j + 1) * high].astype(jnp.int16)


def split_depth(depth):
    main = depth // LANES * LANES
    return main, -(-(depth - main) // 16) * 16


def product(order, where, sources, holes, integrals, own_cols, give_space):
    parts = len(sources)
    _, high_block, depth = sources[0].shape
    part = high_block // parts
    cols = integrals.shape[1]
    rows = own_cols.shape[0]
    width, segments = layout(cols)
    tile = width // segments
    total = len(order) * part
    high = total // (2 * parts)
    main, second = split_depth(depth)
    rest = -(-(second + rows) // LANES) * LANES
    whole = lambda x: pl.BlockSpec(x.shape, lambda i, where: (0,) * x.ndim)
    out = pl.BlockSpec((high, tile), lambda i, where: (0, i))
    return pl.pallas_call(
        functools.partial(product_kernel, order, parts, cols, segments),
        grid_spec=pltpu.PrefetchScalarGridSpec(
            num_scalar_prefetch=1,
            grid=(segments,),
            in_specs=[whole(x) for x in sources]
            + [
                whole(holes),
                pl.BlockSpec((depth, tile), lambda i, where: (0, i)),
                pl.BlockSpec((rows, tile), lambda i, where: (0, i)),
            ],
            out_specs=[out] * (2 * parts),
            scratch_shapes=[
                pltpu.VMEM((total, main), jnp.bfloat16),
                pltpu.VMEM((total, rest), jnp.bfloat16),
                pltpu.VMEM((rest, tile), jnp.bfloat16),
                pltpu.VMEM((total // 2, LANES), jnp.float32),
            ],
        ),
        out_shape=[give_space((high, width), jnp.int16)] * parts
        + [jax.ShapeDtypeStruct((high, width), jnp.float32)] * parts,
        compiler_params=params("arbitrary"),
        cost_estimate=SMALL,
        name="partial_products",
    )(where, *sources, in_hbm(holes), integrals, in_hbm(own_cols))


def add_kernel(cols, segments, inputs, inner, *refs):
    keeps, coded, (give_ref, next_ref) = refs[:inputs], refs[inputs : 2 * inputs], refs[2 * inputs :]
    high, width = next_ref.shape
    half = high // (inputs * inner)
    tile = width // segments
    chunk = min(16, half)

    for index in range(inputs):
        keep_ref, coded_ref = keeps[index], coded[index]

        def total(at, n, codes):
            span = slice(n * tile, (n + 1) * tile)
            return keep_ref[at, span] + decode(coded_ref[at, span], codes, n, cols, n * tile)

        for group in range(inner):
            top, target = 2 * half * group, half * (inner * index + group)

            @pl.loop(0, half // chunk)
            def _(i):
                out = pl.ds(pl.multiple_of(target + i * chunk, chunk), chunk)
                at = pl.ds(pl.multiple_of(top + i * chunk, chunk), chunk)
                codes = codes_of(coded_ref, at, cols, segments)
                made = []
                for n in range(segments):
                    whole, code = encode(total(at, n, codes))
                    made.append(code)
                    if n == segments - 1:
                        whole = with_codes(whole, made, cols, n * tile)
                    give_ref[out, n * tile : (n + 1) * tile] = whole.astype(jnp.int16)

            @pl.loop(0, half // chunk)
            def _(i):
                out = pl.ds(pl.multiple_of(target + i * chunk, chunk), chunk)
                at = pl.ds(pl.multiple_of(top + half + i * chunk, chunk), chunk)
                codes = codes_of(coded_ref, at, cols, segments)
                for n in range(segments):
                    next_ref[out, n * tile : (n + 1) * tile] = total(at, n, codes)


def add(keeps, coded, inner, cols):
    high, width = keeps[0].shape
    out = (len(keeps) * high // 2, width)
    return pl.pallas_call(
        functools.partial(add_kernel, cols, layout(cols)[1], len(keeps), inner),
        out_shape=(
            jax.ShapeDtypeStruct(out, jnp.int16),
            jax.ShapeDtypeStruct(out, jnp.float32),
        ),
        compiler_params=params(),
        cost_estimate=SMALL,
        name="add_partial_sums",
    )(*keeps, *coded)


def update_kernel(cols, segments, inputs, where, *refs):
    keeps, coded, (d_ref, v_ref, o_ref, out_ref) = refs[:inputs], refs[inputs : 2 * inputs], refs[2 * inputs :]
    width = out_ref.shape[1]
    tile = width // segments
    part = out_ref.shape[0] // 2
    for j in range(2):
        keep_ref, coded_ref = keeps[j % inputs], coded[j % inputs]
        at = pl.ds((j // inputs) * part, part)
        here = pl.ds(pl.multiple_of(where[j] * part, part), part)
        mine = pl.ds(pl.multiple_of((where[j] % 2) * part, part), part)
        codes = codes_of(coded_ref, at, cols, segments)
        made = []
        for n in range(segments):
            start, stop = n * tile, (n + 1) * tile
            ladder = keep_ref[at, start:stop]
            ladder = ladder + decode(coded_ref[at, start:stop], codes, n, cols, start)
            driver = d_ref[mine, start : min(stop, cols)].astype(jnp.float32)
            if stop > cols:
                driver = jnp.concatenate(
                    [driver, jnp.zeros((part, stop - cols), jnp.float32)], axis=1
                )
            gap = v_ref[:, start:stop] - o_ref[here, 0:1]
            whole, code = encode((driver + ladder) / gap)
            made.append(code)
            if n == segments - 1:
                whole = with_codes(whole, made, cols, start)
            out_ref[j * part : (j + 1) * part, start:stop] = whole.astype(jnp.int16)


def updated(keeps, coded, driver, pair_energy, hole_energy, where, cols):
    high, width = keeps[0].shape
    high *= len(keeps)
    whole = lambda x: pl.BlockSpec(x.shape, lambda i, where: (0,) * x.ndim)
    return pl.pallas_call(
        functools.partial(update_kernel, cols, layout(cols)[1], len(keeps)),
        grid_spec=pltpu.PrefetchScalarGridSpec(
            num_scalar_prefetch=1,
            grid=(1,),
            in_specs=[whole(x) for x in (*keeps, *coded)]
            + [pl.BlockSpec((high, cols), lambda i, where: (where[0] // 2, 0))]
            + [whole(pair_energy), whole(hole_energy)],
            out_specs=pl.BlockSpec((high, width), lambda i, where: (0, 0)),
        ),
        out_shape=jax.ShapeDtypeStruct((high, width), jnp.int16),
        compiler_params=params("arbitrary"),
        cost_estimate=SMALL,
        name="update_amplitudes",
    )(where, *keeps, *coded, driver, pair_energy, hole_energy)


def place_kernel(cols, segments, groups, where, *refs):
    out_ref, slots = refs[-2:]
    rows = out_ref.shape[0]
    part = rows // 4
    width = refs[0].shape[1]
    tile = width // segments
    for index in range(2 * groups):
        rel, half = index // 2, index % 2
        ref = refs[index]
        group = where[0] ^ rel
        shift = (group * cols) % LANES
        for j in range(2):
            at = pl.ds(j * part, part)
            codes = codes_of(ref, at, cols, segments)
            pieces = [
                decode(ref[at, n * tile : (n + 1) * tile], codes, n, cols, n * tile)
                for n in range(segments)
            ]
            pieces += [jnp.zeros((part, slots.shape[2] - width), jnp.float32)] * (
                slots.shape[2] > width
            )
            x = pltpu.roll(jnp.concatenate(pieces, axis=1), shift, 1)
            quarter = 2 * ((group // 2) % 2 ^ half) + j
            slots[group, pl.ds(pl.multiple_of(quarter * part, part), part), :] = x
    lane = lax.broadcasted_iota(jnp.int32, (rows, LANES), 1)
    for group in range(groups):
        start = group * cols
        base, shift = start // LANES * LANES, start % LANES
        full = (shift + cols) // LANES * LANES
        if group == groups - 1:
            full = shift + cols
        first = 0
        if shift:
            before = (group - 1) * cols % LANES + cols
            before = before // LANES * LANES
            tail = slots[group - 1, :, before : before + LANES]
            out_ref[:, base : base + LANES] = jnp.where(
                lane < shift, tail, slots[group, :, 0:LANES]
            )
            first = LANES
        out_ref[:, base + first : base + full] = slots[group, :, first:full]


def place(blocks, grp, rows, cols, groups):
    width, segments = layout(cols)
    unit = math.gcd(cols, LANES)
    room = width + LANES * (cols % LANES > unit)
    whole = lambda shape: pl.BlockSpec(shape, lambda i, where: (0,) * len(shape))
    out = (rows, groups * cols)
    return pl.pallas_call(
        functools.partial(place_kernel, cols, segments, groups),
        grid_spec=pltpu.PrefetchScalarGridSpec(
            num_scalar_prefetch=1,
            grid=(1,),
            in_specs=[whole(x.shape) for x in blocks],
            out_specs=whole(out),
            scratch_shapes=[pltpu.VMEM((groups, rows, room), jnp.float32)],
        ),
        out_shape=jax.ShapeDtypeStruct(out, jnp.float32),
        compiler_params=params("arbitrary"),
        name="place_columns",
    )(grp, *blocks)


def spans_of(cols, chip):
    first = chip * 2 * cols % LANES
    second = first + cols
    return first, second // LANES, second % LANES, -(-(second + cols) // LANES)


def half_kernel(cols, segments, late, where, *refs):
    coded, refs = refs[:4], refs[4:]
    if late:
        seam_in, _, out_ref, slots, strips, sems = refs
    else:
        out_ref, seam_ref, slots, strips, sems = refs
    high = coded[0].shape[0]
    part = high // 2
    width = coded[0].shape[1]
    tile = width // segments
    for rel, ref in enumerate(coded):
        group = where[0] ^ rel
        for j in range(2):
            at = pl.ds(j * part, part)
            codes = codes_of(ref, at, cols, segments)
            pieces = [
                decode(ref[at, n * tile : (n + 1) * tile], codes, n, cols, n * tile)
                for n in range(segments)
            ]
            x = pltpu.roll(jnp.concatenate(pieces, axis=1), (group * cols) % LANES, 1)
            slots[group, j * part : (j + 1) * part, :] = x
    lane = lax.broadcasted_iota(jnp.int32, (high, LANES), 1)
    stores = []
    for chip in range(2):
        _, turn, shift, tiles = spans_of(cols, chip)
        one, two = slots.at[2 * chip], slots.at[2 * chip + 1]
        strip = strips.at[chip]
        strip[:, : turn * LANES] = one[:, : turn * LANES]
        seam = turn * LANES
        strip[:, seam : seam + LANES] = jnp.where(
            lane < shift, one[:, seam : seam + LANES], two[:, :LANES]
        )
        strip[:, seam + LANES : tiles * LANES] = two[:, LANES : tiles * LANES - seam]
        top = (chip ^ late) * high
        shared = slice(0, LANES) if chip else slice((tiles - 1) * LANES, tiles * LANES)
        if late:
            strip[:, shared] = strip[:, shared] + seam_in[top : top + high, :]
            start, stop = 0, tiles * LANES
        else:
            seam_ref[top : top + high, :] = strip[:, shared]
            start, stop = (LANES, tiles * LANES) if chip else (0, (tiles - 1) * LANES)
        base = chip * 2 * cols // LANES * LANES
        store = pltpu.make_async_copy(
            strip.at[:, start:stop],
            out_ref.at[top : top + high, base + start : base + stop],
            sems.at[chip],
        )
        store.start()
        stores.append(store)
    for store in stores:
        store.wait()


def place_half(blocks, grp, rows, cols, so_far=None):
    width, segments = layout(cols)
    high = rows // 2
    tiles = max(spans_of(cols, chip)[3] for chip in range(2))
    whole = lambda x: pl.BlockSpec(x.shape, lambda i, where: (0,) * x.ndim)
    anywhere = pl.BlockSpec(memory_space=pl.ANY)
    out = jax.ShapeDtypeStruct((rows, 4 * cols), jnp.float32)
    seam = jax.ShapeDtypeStruct((rows, LANES), jnp.float32)
    late = so_far is not None
    return pl.pallas_call(
        functools.partial(half_kernel, cols, segments, late),
        grid_spec=pltpu.PrefetchScalarGridSpec(
            num_scalar_prefetch=1,
            grid=(1,),
            in_specs=[whole(x) for x in blocks] + [whole(seam), anywhere] * late,
            out_specs=anywhere if late else (anywhere, whole(seam)),
            scratch_shapes=[
                pltpu.VMEM((4, high, width), jnp.float32),
                pltpu.VMEM((2, high, tiles * LANES), jnp.float32),
                pltpu.SemaphoreType.DMA((2,)),
            ],
        ),
        out_shape=out if late else (out, seam),
        input_output_aliases={6: 0} if late else {},
        compiler_params=params("arbitrary"),
        name="place_late_half" if late else "place_early_half",
    )(grp, *blocks, *(so_far[::-1] if late else ()))


def shards(amplitudes, integrals, hole_ints, driver, e_occ, e_virt, occ_pairs, virt_pairs):
    groups, pairs = lax.axis_size("grp"), lax.axis_size("pair")
    grp, pair = lax.axis_index("grp"), lax.axis_index("pair")
    rows = amplitudes.shape[0]
    part = rows // 4
    depth, cols = integrals.shape
    width, _ = layout(cols)

    def swap(x, axis, flip):
        size = lax.axis_size(axis)
        return lax.ppermute(x, axis, [(i, i ^ flip) for i in range(size)])

    own_cols = lax.dynamic_slice_in_dim(amplitudes, grp * cols, cols, 1)
    holes = lax.dynamic_slice_in_dim(hole_ints, pair * rows, rows, 1)
    holes = holes.reshape(pairs, 4, part, rows)
    occ_energy = lookup(occ_pairs, e_occ)
    virt_energy = lookup(virt_pairs, e_virt)
    hole_energy = jnp.broadcast_to((occ_energy[0] + occ_energy[1])[:, None], (rows, LANES))
    pair_energy = jnp.pad(
        (virt_energy[0] + virt_energy[1])[None, :],
        ((0, 0), (0, width - cols)),
        constant_values=8.0,
    )

    chip_half, core_at, count = (grp // 2) % 2, grp % 2, pairs // 2
    blocks = list(cut(amplitudes, pair, chip_half, core_at, pairs, depth))
    for j in range(count):
        moves = [
            (g * pairs + p, g * pairs + (p ^ (g % 2 * count + (j + 1) % count)))
            for g in range(groups)
            for p in range(pairs)
        ]
        blocks[j] = lax.ppermute(blocks[j], ("grp", "pair"), moves)
    own = pack(blocks, (own_cols, holes, pair_energy, hole_energy))
    core = pack([swap(x, "grp", 1) for x in blocks], ())
    chip = swap(own, "grp", 2)

    bits = [1 << n for n in range(pairs.bit_length() - 1)]
    x_first, z_first = bits, bits[1::-1] + bits[2:]
    x_then_far = bits[:1] + bits[2:] + bits[1:2]
    routes = ((z_first, x_then_far), (x_then_far, z_first))

    def listed(value, left):
        if not left:
            return [value]
        return listed(value | left[0], left[1:]) + listed(value, left[1:])

    def place_of(half):
        first = 2 * (chip_half ^ half)
        return jnp.stack([first, first + 1])

    def products(half, *sources):
        given = [(q, k) for q, r in enumerate(routes[half]) for k in listed(r[0], r[1:])]
        order = given + [(q, k ^ routes[half][q][0]) for q, k in given]
        where = jnp.concatenate([jnp.stack([pair, core_at]), place_of(half)])
        space = jax.ShapeDtypeStruct if half else pltpu.HBM
        made = product(order, where, sources, holes, integrals, own_cols, space)
        return list(zip(made[:2], made[2:]))

    first = products(0, own, core)
    chip, _ = lax.optimization_barrier((chip, first[0][1]))
    both = swap(chip, "grp", 1)
    second = products(1, chip, both)

    state = [first, second]
    for n in range(len(bits)):
        for half in range(2):
            one, two = routes[half]
            steps = [one[n]] if len(state[half]) == 1 else [one[n], two[n]]
            got = [swap(give, "pair", bit) for (give, _), bit in zip(state[half], steps)]
            keeps = [keep for _, keep in state[half]]
            inner = 3 - len(keeps)
            if n == len(bits) - 1:
                state[half] = (keeps, got)
            elif inner == 2 or one[n + 1 :] == two[n + 1 :]:
                state[half] = [add(keeps, got, inner, cols)]
            else:
                state[half] = [add([k], [g], 1, cols) for k, g in zip(keeps, got)]
    sent = []
    in_halves = groups == 4 and 2 * cols % LANES != 0
    for half in range(2):
        keeps, got = state[half]
        coded = updated(keeps, got, driver, pair_energy, hole_energy, place_of(half), cols)
        here = [coded] + [swap(coded, "grp", 2 * k) for k in range(1, groups // 2)]
        if half and in_halves:
            early = place_half(sent[0], grp[None], rows, cols)
        sent.append([x for own_x in here for x in (own_x, swap(own_x, "grp", 1))])

    if in_halves:
        return place_half(sent[1], grp[None], rows, cols, early)
    ordered = [sent[half][rel] for rel in range(groups) for half in range(2)]
    return place(ordered, grp[None], rows, cols, groups)


def solution(mesh):
    placed = (
        P("pair", None),
        P("pair", "grp"),
        P(),
        P("pair", "grp"),
        P(),
        P(),
        P(None, "pair"),
        P(None, "grp"),
    )
    return jax.shard_map(
        shards, mesh=mesh, in_specs=placed, out_specs=P("pair", None), check_vma=False
    )
```

```python
import functools
import math

import jax
import jax.numpy as jnp
from jax import lax
from jax.experimental import pallas as pl
from jax.experimental.pallas import tpu as pltpu
from jax.sharding import PartitionSpec as P

TOP = 32752.0
STEP = 0.0625
LANES = 128
VMEM_LIMIT = 48 * 1024 * 1024
CUT_LIMIT = 8 * 1024 * 1024
SMALL = pl.CostEstimate(flops=1024, bytes_accessed=1024, transcendentals=0)


def lookup(labels, energies):
    table = lax.broadcasted_iota(jnp.int32, labels.shape + energies.shape, labels.ndim)
    picked = jnp.where(labels[..., None] == table, energies, jnp.float32(0.0))
    return jnp.sum(picked, axis=-1)


def layout(cols):
    width = cols // LANES * LANES + LANES
    tiles = width // LANES
    segments = next(n for n in (3, 2, 1) if tiles % n == 0)
    return width, segments


def columns(rows, size, start):
    return lax.broadcasted_iota(jnp.int32, (rows, size), 1) + start


def encode(x):
    most = jnp.max(jnp.abs(x), axis=1, keepdims=True)
    code = jnp.ceil(jnp.log2(jnp.maximum(most, 1e-30)) * (1.0 / STEP))
    whole = jnp.round(x * (jnp.exp2(code * -STEP) * TOP))
    return whole.astype(jnp.int32), code


def with_codes(whole, codes, cols, start):
    at = columns(whole.shape[0], whole.shape[1], start)
    for n, code in enumerate(codes):
        whole = jnp.where(at == cols + n, code.astype(jnp.int32), whole)
    return whole


def decode(coded, codes, n, cols, start):
    x = coded.astype(jnp.float32) * (jnp.exp2(codes[n] * STEP) * (1.0 / TOP))
    if start + x.shape[1] > cols:
        x = jnp.where(columns(x.shape[0], x.shape[1], start) < cols, x, 0.0)
    return x


def codes_of(coded_ref, at, cols, segments):
    tail = coded_ref[at, cols // LANES * LANES :].astype(jnp.float32)
    first = cols % LANES
    return [tail[:, first + n : first + n + 1] for n in range(segments)]


def in_hbm(x):
    return pltpu.with_memory_space_constraint(x, pltpu.HBM)


def params(*dims, limit=VMEM_LIMIT):
    return pltpu.CompilerParams(
        dimension_semantics=dims or None, vmem_limit_bytes=limit
    )


def cut_kernel(where, a_ref, *refs):
    outs, slots = refs[:-1], refs[-1]
    count, _, depth = slots.shape
    for n in range(2 * count):
        k = where[0] ^ n

        @pl.when(k // count == where[2])
        def _():
            slots[k % count] = a_ref[:, n * depth : (n + 1) * depth]

    for j in range(count):
        outs[j][...] = slots[(j + 1) % count]


def cut(amplitudes, pair, part, core, pairs, depth):
    rows, total = amplitudes.shape
    high, count = rows // 2, pairs // 2
    return pl.pallas_call(
        cut_kernel,
        grid_spec=pltpu.PrefetchScalarGridSpec(
            num_scalar_prefetch=1,
            grid=(1,),
            in_specs=[pl.BlockSpec((high, total), lambda i, where: (where[1], 0))],
            out_specs=[pl.BlockSpec((high, depth), lambda i, where: (0, 0))] * count,
            scratch_shapes=[pltpu.VMEM((count, high, depth), jnp.bfloat16)],
        ),
        out_shape=[jax.ShapeDtypeStruct((high, depth), jnp.bfloat16)] * count,
        compiler_params=params("arbitrary", limit=CUT_LIMIT),
        cost_estimate=SMALL,
        name="cut_blocks",
    )(jnp.stack([pair, part, core]), in_hbm(amplitudes))


def pack_kernel(count, *refs):
    for n in range(count):
        refs[-1][n] = refs[n][...]


def pack(blocks, others):
    shape = (len(blocks),) + blocks[0].shape
    return pl.pallas_call(
        functools.partial(pack_kernel, len(blocks)),
        in_specs=[pl.BlockSpec(memory_space=pltpu.VMEM)] * len(blocks)
        + [pl.BlockSpec(memory_space=pl.ANY)] * len(others),
        out_shape=jax.ShapeDtypeStruct(shape, jnp.bfloat16),
        compiler_params=params(limit=CUT_LIMIT),
        cost_estimate=SMALL,
        name="pack_blocks",
    )(*blocks, *others)


def product_kernel(order, parts, cols, segments, where, *refs):
    a_refs, (h_ref, v_ref, o_ref), outs = refs[:parts], refs[parts : parts + 3], refs[parts + 3 : -4]
    left, left_rest, right_rest, codes = refs[-4:]
    part, depth = a_refs[0].shape[1] // parts, a_refs[0].shape[2]
    rows = o_ref.shape[0]
    main, second = split_depth(depth)
    step = pl.program_id(0)
    tile = v_ref.shape[1]
    high = outs[0].shape[0]

    @pl.when(step == 0)
    def _():
        left_rest[...] = jnp.zeros_like(left_rest)
        right_rest[...] = jnp.zeros_like(right_rest)
        count = a_refs[0].shape[0]
        spot = {entry: n for n, entry in enumerate(order)}
        for s, ref in enumerate(a_refs):
            swapped = where[1] ^ s
            for j in range(count):
                low = (j + 1) % count
                for q in range(parts):
                    near, far = spot[q, low], spot[q, low + count]
                    at = jnp.where(swapped == 0, near, far) * part
                    at = pl.ds(pl.multiple_of(at, part), part)
                    block = ref.at[j, q * part : (q + 1) * part]
                    left[at, :] = block[:, :main]
                    left_rest[at, : depth - main] = block[:, main:]
                    source = where[0] ^ (low + count * swapped)
                    left_rest[at, second : second + rows] = h_ref[source, where[2 + q]]

    right_rest[: depth - main, :] = v_ref[main:, :]
    right_rest[second : second + rows, :] = o_ref[...]
    acc = jnp.dot(left[...], v_ref[:main, :], preferred_element_type=jnp.float32)
    acc = acc + jnp.dot(left_rest[...], right_rest[...], preferred_element_type=jnp.float32)
    acc = jnp.where(columns(acc.shape[0], tile, step * tile) < cols, acc, 0.0)
    given = parts * high
    for j in range(parts):
        outs[parts + j][...] = acc[given + j * high : given + (j + 1) * high]
    whole, code = encode(acc[:given])
    at = lax.broadcasted_iota(jnp.int32, codes.shape, 1)
    codes[...] = jnp.where(at == step, code, codes[...])

    @pl.when(step < segments - 1)
    def _():
        for j in range(parts):
            outs[j][...] = whole[j * high : (j + 1) * high].astype(jnp.int16)

    @pl.when(step == segments - 1)
    def _():
        kept = [codes[:, n : n + 1] for n in range(segments)]
        done = with_codes(whole, kept, cols, (segments - 1) * tile)
        for j in range(parts):
            outs[j][...] = done[j * high : (j + 1) * high].astype(jnp.int16)


def split_depth(depth):
    main = depth // LANES * LANES
    return main, -(-(depth - main) // 16) * 16


def product(order, where, sources, holes, integrals, own_cols, give_space):
    parts = len(sources)
    _, high_block, depth = sources[0].shape
    part = high_block // parts
    cols = integrals.shape[1]
    rows = own_cols.shape[0]
    width, segments = layout(cols)
    tile = width // segments
    total = len(order) * part
    high = total // (2 * parts)
    main, second = split_depth(depth)
    rest = -(-(second + rows) // LANES) * LANES
    whole = lambda x: pl.BlockSpec(x.shape, lambda i, where: (0,) * x.ndim)
    out = pl.BlockSpec((high, tile), lambda i, where: (0, i))
    return pl.pallas_call(
        functools.partial(product_kernel, order, parts, cols, segments),
        grid_spec=pltpu.PrefetchScalarGridSpec(
            num_scalar_prefetch=1,
            grid=(segments,),
            in_specs=[whole(x) for x in sources]
            + [
                whole(holes),
                pl.BlockSpec((depth, tile), lambda i, where: (0, i)),
                pl.BlockSpec((rows, tile), lambda i, where: (0, i)),
            ],
            out_specs=[out] * (2 * parts),
            scratch_shapes=[
                pltpu.VMEM((total, main), jnp.bfloat16),
                pltpu.VMEM((total, rest), jnp.bfloat16),
                pltpu.VMEM((rest, tile), jnp.bfloat16),
                pltpu.VMEM((total // 2, LANES), jnp.float32),
            ],
        ),
        out_shape=[give_space((high, width), jnp.int16)] * parts
        + [jax.ShapeDtypeStruct((high, width), jnp.float32)] * parts,
        compiler_params=params("arbitrary"),
        cost_estimate=SMALL,
        name="partial_products",
    )(where, *sources, in_hbm(holes), integrals, in_hbm(own_cols))


def add_kernel(cols, segments, inputs, inner, *refs):
    keeps, coded, (give_ref, next_ref) = refs[:inputs], refs[inputs : 2 * inputs], refs[2 * inputs :]
    high, width = next_ref.shape
    half = high // (inputs * inner)
    tile = width // segments
    chunk = min(16, half)

    for index in range(inputs):
        keep_ref, coded_ref = keeps[index], coded[index]

        def total(at, n, codes):
            span = slice(n * tile, (n + 1) * tile)
            return keep_ref[at, span] + decode(coded_ref[at, span], codes, n, cols, n * tile)

        for group in range(inner):
            top, target = 2 * half * group, half * (inner * index + group)

            @pl.loop(0, half // chunk)
            def _(i):
                out = pl.ds(pl.multiple_of(target + i * chunk, chunk), chunk)
                at = pl.ds(pl.multiple_of(top + i * chunk, chunk), chunk)
                codes = codes_of(coded_ref, at, cols, segments)
                made = []
                for n in range(segments):
                    whole, code = encode(total(at, n, codes))
                    made.append(code)
                    if n == segments - 1:
                        whole = with_codes(whole, made, cols, n * tile)
                    give_ref[out, n * tile : (n + 1) * tile] = whole.astype(jnp.int16)

            @pl.loop(0, half // chunk)
            def _(i):
                out = pl.ds(pl.multiple_of(target + i * chunk, chunk), chunk)
                at = pl.ds(pl.multiple_of(top + half + i * chunk, chunk), chunk)
                codes = codes_of(coded_ref, at, cols, segments)
                for n in range(segments):
                    next_ref[out, n * tile : (n + 1) * tile] = total(at, n, codes)


def add(keeps, coded, inner, cols):
    high, width = keeps[0].shape
    out = (len(keeps) * high // 2, width)
    return pl.pallas_call(
        functools.partial(add_kernel, cols, layout(cols)[1], len(keeps), inner),
        out_shape=(
            jax.ShapeDtypeStruct(out, jnp.int16),
            jax.ShapeDtypeStruct(out, jnp.float32),
        ),
        compiler_params=params(),
        cost_estimate=SMALL,
        name="add_partial_sums",
    )(*keeps, *coded)


def update_kernel(cols, segments, inputs, where, *refs):
    keeps, coded, (d_ref, v_ref, o_ref, out_ref) = refs[:inputs], refs[inputs : 2 * inputs], refs[2 * inputs :]
    width = out_ref.shape[1]
    tile = width // segments
    part = out_ref.shape[0] // 2
    for j in range(2):
        keep_ref, coded_ref = keeps[j % inputs], coded[j % inputs]
        at = pl.ds((j // inputs) * part, part)
        here = pl.ds(pl.multiple_of(where[j] * part, part), part)
        mine = pl.ds(pl.multiple_of((where[j] % 2) * part, part), part)
        codes = codes_of(coded_ref, at, cols, segments)
        made = []
        for n in range(segments):
            start, stop = n * tile, (n + 1) * tile
            ladder = keep_ref[at, start:stop]
            ladder = ladder + decode(coded_ref[at, start:stop], codes, n, cols, start)
            driver = d_ref[mine, start : min(stop, cols)].astype(jnp.float32)
            if stop > cols:
                driver = jnp.concatenate(
                    [driver, jnp.zeros((part, stop - cols), jnp.float32)], axis=1
                )
            gap = v_ref[:, start:stop] - o_ref[here, 0:1]
            whole, code = encode((driver + ladder) / gap)
            made.append(code)
            if n == segments - 1:
                whole = with_codes(whole, made, cols, start)
            out_ref[j * part : (j + 1) * part, start:stop] = whole.astype(jnp.int16)


def updated(keeps, coded, driver, pair_energy, hole_energy, where, cols):
    high, width = keeps[0].shape
    high *= len(keeps)
    whole = lambda x: pl.BlockSpec(x.shape, lambda i, where: (0,) * x.ndim)
    return pl.pallas_call(
        functools.partial(update_kernel, cols, layout(cols)[1], len(keeps)),
        grid_spec=pltpu.PrefetchScalarGridSpec(
            num_scalar_prefetch=1,
            grid=(1,),
            in_specs=[whole(x) for x in (*keeps, *coded)]
            + [pl.BlockSpec((high, cols), lambda i, where: (where[0] // 2, 0))]
            + [whole(pair_energy), whole(hole_energy)],
            out_specs=pl.BlockSpec((high, width), lambda i, where: (0, 0)),
        ),
        out_shape=jax.ShapeDtypeStruct((high, width), jnp.int16),
        compiler_params=params("arbitrary"),
        cost_estimate=SMALL,
        name="update_amplitudes",
    )(where, *keeps, *coded, driver, pair_energy, hole_energy)


def place_kernel(cols, segments, groups, where, *refs):
    out_ref, slots = refs[-2:]
    rows = out_ref.shape[0]
    part = rows // 4
    width = refs[0].shape[1]
    tile = width // segments
    for index in range(2 * groups):
        rel, half = index // 2, index % 2
        ref = refs[index]
        group = where[0] ^ rel
        shift = (group * cols) % LANES
        for j in range(2):
            at = pl.ds(j * part, part)
            codes = codes_of(ref, at, cols, segments)
            pieces = [
                decode(ref[at, n * tile : (n + 1) * tile], codes, n, cols, n * tile)
                for n in range(segments)
            ]
            pieces += [jnp.zeros((part, slots.shape[2] - width), jnp.float32)] * (
                slots.shape[2] > width
            )
            x = pltpu.roll(jnp.concatenate(pieces, axis=1), shift, 1)
            quarter = 2 * ((group // 2) % 2 ^ half) + j
            slots[group, pl.ds(pl.multiple_of(quarter * part, part), part), :] = x
    lane = lax.broadcasted_iota(jnp.int32, (rows, LANES), 1)
    for group in range(groups):
        start = group * cols
        base, shift = start // LANES * LANES, start % LANES
        full = (shift + cols) // LANES * LANES
        if group == groups - 1:
            full = shift + cols
        first = 0
        if shift:
            before = (group - 1) * cols % LANES + cols
            before = before // LANES * LANES
            tail = slots[group - 1, :, before : before + LANES]
            out_ref[:, base : base + LANES] = jnp.where(
                lane < shift, tail, slots[group, :, 0:LANES]
            )
            first = LANES
        out_ref[:, base + first : base + full] = slots[group, :, first:full]


def place(blocks, grp, rows, cols, groups):
    width, segments = layout(cols)
    unit = math.gcd(cols, LANES)
    room = width + LANES * (cols % LANES > unit)
    whole = lambda shape: pl.BlockSpec(shape, lambda i, where: (0,) * len(shape))
    out = (rows, groups * cols)
    return pl.pallas_call(
        functools.partial(place_kernel, cols, segments, groups),
        grid_spec=pltpu.PrefetchScalarGridSpec(
            num_scalar_prefetch=1,
            grid=(1,),
            in_specs=[whole(x.shape) for x in blocks],
            out_specs=whole(out),
            scratch_shapes=[pltpu.VMEM((groups, rows, room), jnp.float32)],
        ),
        out_shape=jax.ShapeDtypeStruct(out, jnp.float32),
        compiler_params=params("arbitrary"),
        name="place_columns",
    )(grp, *blocks)


def spans_of(cols, chip):
    first = chip * 2 * cols % LANES
    second = first + cols
    return first, second // LANES, second % LANES, -(-(second + cols) // LANES)


def half_kernel(cols, segments, late, where, *refs):
    coded, refs = refs[:4], refs[4:]
    if late:
        seam_in, _, out_ref, slots, strips, sems = refs
    else:
        out_ref, seam_ref, slots, strips, sems = refs
    high = coded[0].shape[0]
    part = high // 2
    width = coded[0].shape[1]
    tile = width // segments
    for rel, ref in enumerate(coded):
        for group in range(4):

            @pl.when(where[0] ^ rel == group)
            def _():
                shift = group * cols % LANES
                for j in range(2):
                    at = slice(j * part, (j + 1) * part)
                    codes = codes_of(ref, at, cols, segments)
                    pieces = [
                        decode(ref[at, n * tile : (n + 1) * tile], codes, n, cols, n * tile)
                        for n in range(segments)
                    ]
                    x = jnp.concatenate(pieces, axis=1)
                    slots[group, at, :] = pltpu.roll(x, shift, 1) if shift else x
    lane = lax.broadcasted_iota(jnp.int32, (high, LANES), 1)
    stores = []
    for chip in range(2):
        _, turn, shift, tiles = spans_of(cols, chip)
        one, two = slots.at[2 * chip], slots.at[2 * chip + 1]
        strip = strips.at[chip]
        strip[:, : turn * LANES] = one[:, : turn * LANES]
        seam = turn * LANES
        strip[:, seam : seam + LANES] = jnp.where(
            lane < shift, one[:, seam : seam + LANES], two[:, :LANES]
        )
        strip[:, seam + LANES : tiles * LANES] = two[:, LANES : tiles * LANES - seam]
        top = (chip ^ late) * high
        shared = slice(0, LANES) if chip else slice((tiles - 1) * LANES, tiles * LANES)
        if late:
            strip[:, shared] = strip[:, shared] + seam_in[top : top + high, :]
            start, stop = 0, tiles * LANES
        else:
            seam_ref[top : top + high, :] = strip[:, shared]
            start, stop = (LANES, tiles * LANES) if chip else (0, (tiles - 1) * LANES)
        base = chip * 2 * cols // LANES * LANES
        store = pltpu.make_async_copy(
            strip.at[:, start:stop],
            out_ref.at[top : top + high, base + start : base + stop],
            sems.at[chip],
        )
        store.start()
        stores.append(store)
    for store in stores:
        store.wait()


def place_half(blocks, grp, rows, cols, so_far=None):
    width, segments = layout(cols)
    high = rows // 2
    tiles = max(spans_of(cols, chip)[3] for chip in range(2))
    whole = lambda x: pl.BlockSpec(x.shape, lambda i, where: (0,) * x.ndim)
    anywhere = pl.BlockSpec(memory_space=pl.ANY)
    out = jax.ShapeDtypeStruct((rows, 4 * cols), jnp.float32)
    seam = jax.ShapeDtypeStruct((rows, LANES), jnp.float32)
    late = so_far is not None
    return pl.pallas_call(
        functools.partial(half_kernel, cols, segments, late),
        grid_spec=pltpu.PrefetchScalarGridSpec(
            num_scalar_prefetch=1,
            grid=(1,),
            in_specs=[whole(x) for x in blocks] + [whole(seam), anywhere] * late,
            out_specs=anywhere if late else (anywhere, whole(seam)),
            scratch_shapes=[
                pltpu.VMEM((4, high, width), jnp.float32),
                pltpu.VMEM((2, high, tiles * LANES), jnp.float32),
                pltpu.SemaphoreType.DMA((2,)),
            ],
        ),
        out_shape=out if late else (out, seam),
        input_output_aliases={6: 0} if late else {},
        compiler_params=params("arbitrary"),
        name="place_late_half" if late else "place_early_half",
    )(grp, *blocks, *(so_far[::-1] if late else ()))


def shards(amplitudes, integrals, hole_ints, driver, e_occ, e_virt, occ_pairs, virt_pairs):
    groups, pairs = lax.axis_size("grp"), lax.axis_size("pair")
    grp, pair = lax.axis_index("grp"), lax.axis_index("pair")
    rows = amplitudes.shape[0]
    part = rows // 4
    depth, cols = integrals.shape
    width, _ = layout(cols)

    def swap(x, axis, flip):
        size = lax.axis_size(axis)
        return lax.ppermute(x, axis, [(i, i ^ flip) for i in range(size)])

    own_cols = lax.dynamic_slice_in_dim(amplitudes, grp * cols, cols, 1)
    holes = lax.dynamic_slice_in_dim(hole_ints, pair * rows, rows, 1)
    holes = holes.reshape(pairs, 4, part, rows)
    occ_energy = lookup(occ_pairs, e_occ)
    virt_energy = lookup(virt_pairs, e_virt)
    hole_energy = jnp.broadcast_to((occ_energy[0] + occ_energy[1])[:, None], (rows, LANES))
    pair_energy = jnp.pad(
        (virt_energy[0] + virt_energy[1])[None, :],
        ((0, 0), (0, width - cols)),
        constant_values=8.0,
    )

    chip_half, core_at, count = (grp // 2) % 2, grp % 2, pairs // 2
    blocks = list(cut(amplitudes, pair, chip_half, core_at, pairs, depth))
    for j in range(count):
        moves = [
            (g * pairs + p, g * pairs + (p ^ (g % 2 * count + (j + 1) % count)))
            for g in range(groups)
            for p in range(pairs)
        ]
        blocks[j] = lax.ppermute(blocks[j], ("grp", "pair"), moves)
    own = pack(blocks, (own_cols, holes, pair_energy, hole_energy))
    core = pack([swap(x, "grp", 1) for x in blocks], ())
    chip = swap(own, "grp", 2)

    bits = [1 << n for n in range(pairs.bit_length() - 1)]
    x_first, z_first = bits, bits[1::-1] + bits[2:]
    x_then_far = bits[:1] + bits[2:] + bits[1:2]
    routes = ((z_first, x_then_far), (z_first, x_first))

    def listed(value, left):
        if not left:
            return [value]
        return listed(value | left[0], left[1:]) + listed(value, left[1:])

    def place_of(half):
        first = 2 * (chip_half ^ half)
        return jnp.stack([first, first + 1])

    def products(half, *sources):
        given = [(q, k) for q, r in enumerate(routes[half]) for k in listed(r[0], r[1:])]
        order = given + [(q, k ^ routes[half][q][0]) for q, k in given]
        where = jnp.concatenate([jnp.stack([pair, core_at]), place_of(half)])
        space = jax.ShapeDtypeStruct if half else pltpu.HBM
        made = product(order, where, sources, holes, integrals, own_cols, space)
        return list(zip(made[:2], made[2:]))

    first = products(0, own, core)
    chip, _ = lax.optimization_barrier((chip, first[0][1]))
    both = swap(chip, "grp", 1)
    second = products(1, chip, both)

    state = [first, second]
    for n in range(len(bits)):
        for half in range(2):
            one, two = routes[half]
            steps = [one[n]] if len(state[half]) == 1 else [one[n], two[n]]
            got = [swap(give, "pair", bit) for (give, _), bit in zip(state[half], steps)]
            keeps = [keep for _, keep in state[half]]
            inner = 3 - len(keeps)
            if n == len(bits) - 1:
                state[half] = (keeps, got)
            elif inner == 2:
                state[half] = [add(keeps, got, inner, cols)]
            else:
                state[half] = [add([k], [g], 1, cols) for k, g in zip(keeps, got)]
    sent = []
    in_halves = groups == 4 and 2 * cols % LANES != 0
    for half in range(2):
        keeps, got = state[half]
        coded = updated(keeps, got, driver, pair_energy, hole_energy, place_of(half), cols)
        here = [coded] + [swap(coded, "grp", 2 * k) for k in range(1, groups // 2)]
        if half and in_halves:
            early = place_half(sent[0], grp[None], rows, cols)
        sent.append([x for own_x in here for x in (own_x, swap(own_x, "grp", 1))])

    if in_halves:
        return place_half(sent[1], grp[None], rows, cols, early)
    ordered = [sent[half][rel] for rel in range(groups) for half in range(2)]
    return place(ordered, grp[None], rows, cols, groups)


def solution(mesh):
    placed = (
        P("pair", None),
        P("pair", "grp"),
        P(),
        P("pair", "grp"),
        P(),
        P(),
        P(None, "pair"),
        P(None, "grp"),
    )
    return jax.shard_map(
        shards, mesh=mesh, in_specs=placed, out_specs=P("pair", None), check_vma=False
    )
```

```python
import functools
import math

import jax
import jax.numpy as jnp
from jax import lax
from jax.experimental import pallas as pl
from jax.experimental.pallas import tpu as pltpu
from jax.sharding import PartitionSpec as P

TOP = 32752.0
STEP = 0.0625
LANES = 128
VMEM_LIMIT = 48 * 1024 * 1024
CUT_LIMIT = 8 * 1024 * 1024
SMALL = pl.CostEstimate(flops=1024, bytes_accessed=1024, transcendentals=0)


def lookup(labels, energies):
    table = lax.broadcasted_iota(jnp.int32, labels.shape + energies.shape, labels.ndim)
    picked = jnp.where(labels[..., None] == table, energies, jnp.float32(0.0))
    return jnp.sum(picked, axis=-1)


def layout(cols):
    width = cols // LANES * LANES + LANES
    tiles = width // LANES
    segments = next(n for n in (3, 2, 1) if tiles % n == 0)
    return width, segments


def columns(rows, size, start):
    return lax.broadcasted_iota(jnp.int32, (rows, size), 1) + start


def encode(x):
    most = jnp.max(jnp.abs(x), axis=1, keepdims=True)
    code = jnp.ceil(jnp.log2(jnp.maximum(most, 1e-30)) * (1.0 / STEP))
    whole = jnp.round(x * (jnp.exp2(code * -STEP) * TOP))
    return whole.astype(jnp.int32), code


def with_codes(whole, codes, cols, start):
    at = columns(whole.shape[0], whole.shape[1], start)
    for n, code in enumerate(codes):
        whole = jnp.where(at == cols + n, code.astype(jnp.int32), whole)
    return whole


def decode(coded, codes, n, cols, start):
    x = coded.astype(jnp.float32) * (jnp.exp2(codes[n] * STEP) * (1.0 / TOP))
    if start + x.shape[1] > cols:
        x = jnp.where(columns(x.shape[0], x.shape[1], start) < cols, x, 0.0)
    return x


def codes_of(coded_ref, at, cols, segments):
    tail = coded_ref[at, cols // LANES * LANES :].astype(jnp.float32)
    first = cols % LANES
    return [tail[:, first + n : first + n + 1] for n in range(segments)]


def in_hbm(x):
    return pltpu.with_memory_space_constraint(x, pltpu.HBM)


def params(*dims, limit=VMEM_LIMIT):
    return pltpu.CompilerParams(
        dimension_semantics=dims or None, vmem_limit_bytes=limit
    )


def cut_kernel(where, a_ref, *refs):
    outs, slots = refs[:-1], refs[-1]
    count, _, depth = slots.shape
    for n in range(2 * count):
        k = where[0] ^ n

        @pl.when(k // count == where[2])
        def _():
            slots[k % count] = a_ref[:, n * depth : (n + 1) * depth]

    for j in range(count):
        outs[j][...] = slots[(j + 1) % count]


def cut(amplitudes, pair, part, core, pairs, depth):
    rows, total = amplitudes.shape
    high, count = rows // 2, pairs // 2
    return pl.pallas_call(
        cut_kernel,
        grid_spec=pltpu.PrefetchScalarGridSpec(
            num_scalar_prefetch=1,
            grid=(1,),
            in_specs=[pl.BlockSpec((high, total), lambda i, where: (where[1], 0))],
            out_specs=[pl.BlockSpec((high, depth), lambda i, where: (0, 0))] * count,
            scratch_shapes=[pltpu.VMEM((count, high, depth), jnp.bfloat16)],
        ),
        out_shape=[jax.ShapeDtypeStruct((high, depth), jnp.bfloat16)] * count,
        compiler_params=params("arbitrary", limit=CUT_LIMIT),
        cost_estimate=SMALL,
        name="cut_blocks",
    )(jnp.stack([pair, part, core]), in_hbm(amplitudes))


def pack_kernel(count, *refs):
    for n in range(count):
        refs[-1][n] = refs[n][...]


def pack(blocks, others):
    shape = (len(blocks),) + blocks[0].shape
    return pl.pallas_call(
        functools.partial(pack_kernel, len(blocks)),
        in_specs=[pl.BlockSpec(memory_space=pltpu.VMEM)] * len(blocks)
        + [pl.BlockSpec(memory_space=pl.ANY)] * len(others),
        out_shape=jax.ShapeDtypeStruct(shape, jnp.bfloat16),
        compiler_params=params(limit=CUT_LIMIT),
        cost_estimate=SMALL,
        name="pack_blocks",
    )(*blocks, *others)


def product_kernel(order, parts, cols, segments, where, *refs):
    a_refs, (h_ref, v_ref, o_ref), outs = refs[:parts], refs[parts : parts + 3], refs[parts + 3 : -4]
    left, left_rest, right_rest, codes = refs[-4:]
    part, depth = a_refs[0].shape[1] // parts, a_refs[0].shape[2]
    rows = o_ref.shape[0]
    main, second = split_depth(depth)
    step = pl.program_id(0)
    tile = v_ref.shape[1]
    high = outs[0].shape[0]

    @pl.when(step == 0)
    def _():
        left_rest[...] = jnp.zeros_like(left_rest)
        right_rest[...] = jnp.zeros_like(right_rest)
        count = a_refs[0].shape[0]
        spot = {entry: n for n, entry in enumerate(order)}
        for s, ref in enumerate(a_refs):
            swapped = where[1] ^ s
            for j in range(count):
                low = (j + 1) % count
                for q in range(parts):
                    near, far = spot[q, low], spot[q, low + count]
                    at = jnp.where(swapped == 0, near, far) * part
                    at = pl.ds(pl.multiple_of(at, part), part)
                    block = ref.at[j, q * part : (q + 1) * part]
                    left[at, :] = block[:, :main]
                    left_rest[at, : depth - main] = block[:, main:]
                    source = where[0] ^ (low + count * swapped)
                    left_rest[at, second : second + rows] = h_ref[source, where[2 + q]]

    right_rest[: depth - main, :] = v_ref[main:, :]
    right_rest[second : second + rows, :] = o_ref[...]
    acc = jnp.dot(left[...], v_ref[:main, :], preferred_element_type=jnp.float32)
    acc = acc + jnp.dot(left_rest[...], right_rest[...], preferred_element_type=jnp.float32)
    acc = jnp.where(columns(acc.shape[0], tile, step * tile) < cols, acc, 0.0)
    given = parts * high
    for j in range(parts):
        outs[parts + j][...] = acc[given + j * high : given + (j + 1) * high]
    whole, code = encode(acc[:given])
    at = lax.broadcasted_iota(jnp.int32, codes.shape, 1)
    codes[...] = jnp.where(at == step, code, codes[...])

    @pl.when(step < segments - 1)
    def _():
        for j in range(parts):
            outs[j][...] = whole[j * high : (j + 1) * high].astype(jnp.int16)

    @pl.when(step == segments - 1)
    def _():
        kept = [codes[:, n : n + 1] for n in range(segments)]
        done = with_codes(whole, kept, cols, (segments - 1) * tile)
        for j in range(parts):
            outs[j][...] = done[j * high : (j + 1) * high].astype(jnp.int16)


def split_depth(depth):
    main = depth // LANES * LANES
    return main, -(-(depth - main) // 16) * 16


def product(order, where, sources, holes, integrals, own_cols, give_space):
    parts = len(sources)
    _, high_block, depth = sources[0].shape
    part = high_block // parts
    cols = integrals.shape[1]
    rows = own_cols.shape[0]
    width, segments = layout(cols)
    tile = width // segments
    total = len(order) * part
    high = total // (2 * parts)
    main, second = split_depth(depth)
    rest = -(-(second + rows) // LANES) * LANES
    whole = lambda x: pl.BlockSpec(x.shape, lambda i, where: (0,) * x.ndim)
    out = pl.BlockSpec((high, tile), lambda i, where: (0, i))
    return pl.pallas_call(
        functools.partial(product_kernel, order, parts, cols, segments),
        grid_spec=pltpu.PrefetchScalarGridSpec(
            num_scalar_prefetch=1,
            grid=(segments,),
            in_specs=[whole(x) for x in sources]
            + [
                whole(holes),
                pl.BlockSpec((depth, tile), lambda i, where: (0, i)),
                pl.BlockSpec((rows, tile), lambda i, where: (0, i)),
            ],
            out_specs=[out] * (2 * parts),
            scratch_shapes=[
                pltpu.VMEM((total, main), jnp.bfloat16),
                pltpu.VMEM((total, rest), jnp.bfloat16),
                pltpu.VMEM((rest, tile), jnp.bfloat16),
                pltpu.VMEM((total // 2, LANES), jnp.float32),
            ],
        ),
        out_shape=[give_space((high, width), jnp.int16)] * parts
        + [jax.ShapeDtypeStruct((high, width), jnp.float32)] * parts,
        compiler_params=params("arbitrary"),
        cost_estimate=SMALL,
        name="partial_products",
    )(where, *sources, in_hbm(holes), integrals, in_hbm(own_cols))


def add_kernel(cols, segments, inputs, inner, *refs):
    keeps, coded, (give_ref, next_ref) = refs[:inputs], refs[inputs : 2 * inputs], refs[2 * inputs :]
    high, width = next_ref.shape
    half = high // (inputs * inner)
    tile = width // segments
    chunk = min(16, half)

    for index in range(inputs):
        keep_ref, coded_ref = keeps[index], coded[index]

        def total(at, n, codes):
            span = slice(n * tile, (n + 1) * tile)
            return keep_ref[at, span] + decode(coded_ref[at, span], codes, n, cols, n * tile)

        for group in range(inner):
            top, target = 2 * half * group, half * (inner * index + group)

            @pl.loop(0, half // chunk)
            def _(i):
                out = pl.ds(pl.multiple_of(target + i * chunk, chunk), chunk)
                at = pl.ds(pl.multiple_of(top + i * chunk, chunk), chunk)
                codes = codes_of(coded_ref, at, cols, segments)
                made = []
                for n in range(segments):
                    whole, code = encode(total(at, n, codes))
                    made.append(code)
                    if n == segments - 1:
                        whole = with_codes(whole, made, cols, n * tile)
                    give_ref[out, n * tile : (n + 1) * tile] = whole.astype(jnp.int16)

            @pl.loop(0, half // chunk)
            def _(i):
                out = pl.ds(pl.multiple_of(target + i * chunk, chunk), chunk)
                at = pl.ds(pl.multiple_of(top + half + i * chunk, chunk), chunk)
                codes = codes_of(coded_ref, at, cols, segments)
                for n in range(segments):
                    next_ref[out, n * tile : (n + 1) * tile] = total(at, n, codes)


def add(keeps, coded, inner, cols):
    high, width = keeps[0].shape
    out = (len(keeps) * high // 2, width)
    return pl.pallas_call(
        functools.partial(add_kernel, cols, layout(cols)[1], len(keeps), inner),
        out_shape=(
            jax.ShapeDtypeStruct(out, jnp.int16),
            jax.ShapeDtypeStruct(out, jnp.float32),
        ),
        compiler_params=params(),
        cost_estimate=SMALL,
        name="add_partial_sums",
    )(*keeps, *coded)


def update_kernel(cols, segments, inputs, where, *refs):
    keeps, coded, (d_ref, v_ref, o_ref, out_ref) = refs[:inputs], refs[inputs : 2 * inputs], refs[2 * inputs :]
    width = out_ref.shape[1]
    tile = width // segments
    part = out_ref.shape[0] // 2
    for j in range(2):
        keep_ref, coded_ref = keeps[j % inputs], coded[j % inputs]
        at = pl.ds((j // inputs) * part, part)
        here = pl.ds(pl.multiple_of(where[j] * part, part), part)
        mine = pl.ds(pl.multiple_of((where[j] % 2) * part, part), part)
        codes = codes_of(coded_ref, at, cols, segments)
        made = []
        for n in range(segments):
            start, stop = n * tile, (n + 1) * tile
            ladder = keep_ref[at, start:stop]
            ladder = ladder + decode(coded_ref[at, start:stop], codes, n, cols, start)
            driver = d_ref[mine, start : min(stop, cols)].astype(jnp.float32)
            if stop > cols:
                driver = jnp.concatenate(
                    [driver, jnp.zeros((part, stop - cols), jnp.float32)], axis=1
                )
            gap = v_ref[:, start:stop] - o_ref[here, 0:1]
            whole, code = encode((driver + ladder) / gap)
            made.append(code)
            if n == segments - 1:
                whole = with_codes(whole, made, cols, start)
            out_ref[j * part : (j + 1) * part, start:stop] = whole.astype(jnp.int16)


def updated(keeps, coded, driver, pair_energy, hole_energy, where, cols):
    high, width = keeps[0].shape
    high *= len(keeps)
    whole = lambda x: pl.BlockSpec(x.shape, lambda i, where: (0,) * x.ndim)
    return pl.pallas_call(
        functools.partial(update_kernel, cols, layout(cols)[1], len(keeps)),
        grid_spec=pltpu.PrefetchScalarGridSpec(
            num_scalar_prefetch=1,
            grid=(1,),
            in_specs=[whole(x) for x in (*keeps, *coded)]
            + [pl.BlockSpec((high, cols), lambda i, where: (where[0] // 2, 0))]
            + [whole(pair_energy), whole(hole_energy)],
            out_specs=pl.BlockSpec((high, width), lambda i, where: (0, 0)),
        ),
        out_shape=jax.ShapeDtypeStruct((high, width), jnp.int16),
        compiler_params=params("arbitrary"),
        cost_estimate=SMALL,
        name="update_amplitudes",
    )(where, *keeps, *coded, driver, pair_energy, hole_energy)


def place_kernel(cols, segments, groups, where, *refs):
    out_ref, slots = refs[-2:]
    rows = out_ref.shape[0]
    part = rows // 4
    width = refs[0].shape[1]
    tile = width // segments
    for index in range(2 * groups):
        rel, half = index // 2, index % 2
        ref = refs[index]
        group = where[0] ^ rel
        shift = (group * cols) % LANES
        for j in range(2):
            at = pl.ds(j * part, part)
            codes = codes_of(ref, at, cols, segments)
            pieces = [
                decode(ref[at, n * tile : (n + 1) * tile], codes, n, cols, n * tile)
                for n in range(segments)
            ]
            pieces += [jnp.zeros((part, slots.shape[2] - width), jnp.float32)] * (
                slots.shape[2] > width
            )
            x = pltpu.roll(jnp.concatenate(pieces, axis=1), shift, 1)
            quarter = 2 * ((group // 2) % 2 ^ half) + j
            slots[group, pl.ds(pl.multiple_of(quarter * part, part), part), :] = x
    lane = lax.broadcasted_iota(jnp.int32, (rows, LANES), 1)
    for group in range(groups):
        start = group * cols
        base, shift = start // LANES * LANES, start % LANES
        full = (shift + cols) // LANES * LANES
        if group == groups - 1:
            full = shift + cols
        first = 0
        if shift:
            before = (group - 1) * cols % LANES + cols
            before = before // LANES * LANES
            tail = slots[group - 1, :, before : before + LANES]
            out_ref[:, base : base + LANES] = jnp.where(
                lane < shift, tail, slots[group, :, 0:LANES]
            )
            first = LANES
        out_ref[:, base + first : base + full] = slots[group, :, first:full]


def place(blocks, grp, rows, cols, groups):
    width, segments = layout(cols)
    unit = math.gcd(cols, LANES)
    room = width + LANES * (cols % LANES > unit)
    whole = lambda shape: pl.BlockSpec(shape, lambda i, where: (0,) * len(shape))
    out = (rows, groups * cols)
    return pl.pallas_call(
        functools.partial(place_kernel, cols, segments, groups),
        grid_spec=pltpu.PrefetchScalarGridSpec(
            num_scalar_prefetch=1,
            grid=(1,),
            in_specs=[whole(x.shape) for x in blocks],
            out_specs=whole(out),
            scratch_shapes=[pltpu.VMEM((groups, rows, room), jnp.float32)],
        ),
        out_shape=jax.ShapeDtypeStruct(out, jnp.float32),
        compiler_params=params("arbitrary"),
        name="place_columns",
    )(grp, *blocks)


def spans_of(cols, chip):
    first = chip * 2 * cols % LANES
    second = first + cols
    return first, second // LANES, second % LANES, -(-(second + cols) // LANES)


def half_kernel(cols, segments, late, where, *refs):
    coded, refs = refs[:4], refs[4:]
    if late:
        seam_in, _, out_ref, slots, strips, sems = refs
    else:
        out_ref, seam_ref, slots, strips, sems = refs
    high = coded[0].shape[0]
    part = high // 2
    width = coded[0].shape[1]
    tile = width // segments
    for rel, ref in enumerate(coded):
        for group in range(4):

            @pl.when(where[0] ^ rel == group)
            def _():
                shift = group * cols % LANES
                for j in range(2):
                    at = slice(j * part, (j + 1) * part)
                    codes = codes_of(ref, at, cols, segments)
                    pieces = [
                        decode(ref[at, n * tile : (n + 1) * tile], codes, n, cols, n * tile)
                        for n in range(segments)
                    ]
                    x = jnp.concatenate(pieces, axis=1)
                    slots[group, at, :] = pltpu.roll(x, shift, 1) if shift else x
    lane = lax.broadcasted_iota(jnp.int32, (high, LANES), 1)
    stores = []
    for chip in range(2):
        _, turn, shift, tiles = spans_of(cols, chip)
        one, two = slots.at[2 * chip], slots.at[2 * chip + 1]
        strip = strips.at[chip]
        strip[:, : turn * LANES] = one[:, : turn * LANES]
        seam = turn * LANES
        strip[:, seam : seam + LANES] = jnp.where(
            lane < shift, one[:, seam : seam + LANES], two[:, :LANES]
        )
        strip[:, seam + LANES : tiles * LANES] = two[:, LANES : tiles * LANES - seam]
        top = (chip ^ late) * high
        shared = slice(0, LANES) if chip else slice((tiles - 1) * LANES, tiles * LANES)
        if late:
            strip[:, shared] = strip[:, shared] + seam_in[top : top + high, :]
            start, stop = 0, tiles * LANES
        else:
            seam_ref[top : top + high, :] = strip[:, shared]
            start, stop = (LANES, tiles * LANES) if chip else (0, (tiles - 1) * LANES)
        base = chip * 2 * cols // LANES * LANES
        store = pltpu.make_async_copy(
            strip.at[:, start:stop],
            out_ref.at[top : top + high, base + start : base + stop],
            sems.at[chip],
        )
        store.start()
        stores.append(store)
    for store in stores:
        store.wait()


def place_half(blocks, grp, rows, cols, so_far=None):
    width, segments = layout(cols)
    high = rows // 2
    tiles = max(spans_of(cols, chip)[3] for chip in range(2))
    whole = lambda x: pl.BlockSpec(x.shape, lambda i, where: (0,) * x.ndim)
    anywhere = pl.BlockSpec(memory_space=pl.ANY)
    out = jax.ShapeDtypeStruct((rows, 4 * cols), jnp.float32)
    seam = jax.ShapeDtypeStruct((rows, LANES), jnp.float32)
    late = so_far is not None
    return pl.pallas_call(
        functools.partial(half_kernel, cols, segments, late),
        grid_spec=pltpu.PrefetchScalarGridSpec(
            num_scalar_prefetch=1,
            grid=(1,),
            in_specs=[whole(x) for x in blocks] + [whole(seam), anywhere] * late,
            out_specs=anywhere if late else (anywhere, whole(seam)),
            scratch_shapes=[
                pltpu.VMEM((4, high, width), jnp.float32),
                pltpu.VMEM((2, high, tiles * LANES), jnp.float32),
                pltpu.SemaphoreType.DMA((2,)),
            ],
        ),
        out_shape=out if late else (out, seam),
        input_output_aliases={6: 0} if late else {},
        compiler_params=params("arbitrary"),
        name="place_late_half" if late else "place_early_half",
    )(grp, *blocks, *(so_far[::-1] if late else ()))


def shards(amplitudes, integrals, hole_ints, driver, e_occ, e_virt, occ_pairs, virt_pairs):
    groups, pairs = lax.axis_size("grp"), lax.axis_size("pair")
    grp, pair = lax.axis_index("grp"), lax.axis_index("pair")
    rows = amplitudes.shape[0]
    part = rows // 4
    depth, cols = integrals.shape
    width, _ = layout(cols)

    def swap(x, axis, flip):
        size = lax.axis_size(axis)
        return lax.ppermute(x, axis, [(i, i ^ flip) for i in range(size)])

    own_cols = lax.dynamic_slice_in_dim(amplitudes, grp * cols, cols, 1)
    holes = lax.dynamic_slice_in_dim(hole_ints, pair * rows, rows, 1)
    holes = holes.reshape(pairs, 4, part, rows)
    chip_half, core_at, count = (grp // 2) % 2, grp % 2, pairs // 2
    blocks = list(cut(amplitudes, pair, chip_half, core_at, pairs, depth))
    for j in range(count):
        moves = [
            (g * pairs + p, g * pairs + (p ^ (g % 2 * count + (j + 1) % count)))
            for g in range(groups)
            for p in range(pairs)
        ]
        blocks[j] = lax.ppermute(blocks[j], ("grp", "pair"), moves)
    own = pack(blocks, (own_cols, holes))
    core = pack([swap(x, "grp", 1) for x in blocks], ())
    chip = swap(own, "grp", 2)

    bits = [1 << n for n in range(pairs.bit_length() - 1)]
    x_first, z_first = bits, bits[1::-1] + bits[2:]
    x_then_far = bits[:1] + bits[2:] + bits[1:2]
    routes = ((z_first, x_then_far), (z_first, x_first))

    def listed(value, left):
        if not left:
            return [value]
        return listed(value | left[0], left[1:]) + listed(value, left[1:])

    def place_of(half):
        first = 2 * (chip_half ^ half)
        return jnp.stack([first, first + 1])

    def products(half, *sources):
        given = [(q, k) for q, r in enumerate(routes[half]) for k in listed(r[0], r[1:])]
        order = given + [(q, k ^ routes[half][q][0]) for q, k in given]
        where = jnp.concatenate([jnp.stack([pair, core_at]), place_of(half)])
        space = jax.ShapeDtypeStruct if half else pltpu.HBM
        made = product(order, where, sources, holes, integrals, own_cols, space)
        return list(zip(made[:2], made[2:]))

    first = products(0, own, core)
    chip, _ = lax.optimization_barrier((chip, first[0][1]))
    both = swap(chip, "grp", 1)
    second = products(1, chip, both)

    state = [first, second]
    for n in range(len(bits)):
        for half in range(2):
            one, two = routes[half]
            steps = [one[n]] if len(state[half]) == 1 else [one[n], two[n]]
            got = [swap(give, "pair", bit) for (give, _), bit in zip(state[half], steps)]
            keeps = [keep for _, keep in state[half]]
            inner = 3 - len(keeps)
            if n == 0 and half == 0:
                after_first = got[0]
            if n == len(bits) - 1:
                state[half] = (keeps, got)
            elif inner == 2:
                state[half] = [add(keeps, got, inner, cols)]
            else:
                state[half] = [add([k], [g], 1, cols) for k, g in zip(keeps, got)]
    (occ_pairs, virt_pairs), _ = lax.optimization_barrier(
        ((occ_pairs, virt_pairs), after_first)
    )
    occ_energy = lookup(occ_pairs, e_occ)
    virt_energy = lookup(virt_pairs, e_virt)
    hole_energy = jnp.broadcast_to((occ_energy[0] + occ_energy[1])[:, None], (rows, LANES))
    pair_energy = jnp.pad(
        (virt_energy[0] + virt_energy[1])[None, :],
        ((0, 0), (0, width - cols)),
        constant_values=8.0,
    )

    sent = []
    in_halves = groups == 4 and 2 * cols % LANES != 0
    for half in range(2):
        keeps, got = state[half]
        coded = updated(keeps, got, driver, pair_energy, hole_energy, place_of(half), cols)
        here = [coded] + [swap(coded, "grp", 2 * k) for k in range(1, groups // 2)]
        if half and in_halves:
            early = place_half(sent[0], grp[None], rows, cols)
        sent.append([x for own_x in here for x in (own_x, swap(own_x, "grp", 1))])

    if in_halves:
        return place_half(sent[1], grp[None], rows, cols, early)
    ordered = [sent[half][rel] for rel in range(groups) for half in range(2)]
    return place(ordered, grp[None], rows, cols, groups)


def solution(mesh):
    placed = (
        P("pair", None),
        P("pair", "grp"),
        P(),
        P("pair", "grp"),
        P(),
        P(),
        P(None, "pair"),
        P(None, "grp"),
    )
    return jax.shard_map(
        shards, mesh=mesh, in_specs=placed, out_specs=P("pair", None), check_vma=False
    )
```

```python
import functools
import math

import jax
import jax.numpy as jnp
from jax import lax
from jax.experimental import pallas as pl
from jax.experimental.pallas import tpu as pltpu
from jax.sharding import PartitionSpec as P

TOP = 32752.0
STEP = 0.0625
LANES = 128
VMEM_LIMIT = 48 * 1024 * 1024
CUT_LIMIT = 8 * 1024 * 1024
SMALL = pl.CostEstimate(flops=1024, bytes_accessed=1024, transcendentals=0)


def lookup(labels, energies):
    table = lax.broadcasted_iota(jnp.int32, labels.shape + energies.shape, labels.ndim)
    picked = jnp.where(labels[..., None] == table, energies, jnp.float32(0.0))
    return jnp.sum(picked, axis=-1)


def layout(cols):
    width = cols // LANES * LANES + LANES
    tiles = width // LANES
    segments = next(n for n in (3, 2, 1) if tiles % n == 0)
    return width, segments


def columns(rows, size, start):
    return lax.broadcasted_iota(jnp.int32, (rows, size), 1) + start


def encode(x):
    most = jnp.max(jnp.abs(x), axis=1, keepdims=True)
    code = jnp.ceil(jnp.log2(jnp.maximum(most, 1e-30)) * (1.0 / STEP))
    whole = jnp.round(x * (jnp.exp2(code * -STEP) * TOP))
    return whole.astype(jnp.int32), code


def with_codes(whole, codes, cols, start):
    at = columns(whole.shape[0], whole.shape[1], start)
    for n, code in enumerate(codes):
        whole = jnp.where(at == cols + n, code.astype(jnp.int32), whole)
    return whole


def decode(coded, codes, n, cols, start):
    x = coded.astype(jnp.float32) * (jnp.exp2(codes[n] * STEP) * (1.0 / TOP))
    if start + x.shape[1] > cols:
        x = jnp.where(columns(x.shape[0], x.shape[1], start) < cols, x, 0.0)
    return x


def codes_of(coded_ref, at, cols, segments):
    tail = coded_ref[at, cols // LANES * LANES :].astype(jnp.float32)
    first = cols % LANES
    return [tail[:, first + n : first + n + 1] for n in range(segments)]


def in_hbm(x):
    return pltpu.with_memory_space_constraint(x, pltpu.HBM)


def params(*dims, limit=VMEM_LIMIT):
    return pltpu.CompilerParams(
        dimension_semantics=dims or None, vmem_limit_bytes=limit
    )


def cut_kernel(where, a_ref, *refs):
    outs, slots = refs[:-1], refs[-1]
    count, _, depth = slots.shape
    for n in range(2 * count):
        k = where[0] ^ n

        @pl.when(k // count == where[2])
        def _():
            slots[k % count] = a_ref[:, n * depth : (n + 1) * depth]

    for j in range(count):
        outs[j][...] = slots[(j + 1) % count]


def cut(amplitudes, pair, part, core, pairs, depth):
    rows, total = amplitudes.shape
    high, count = rows // 2, pairs // 2
    return pl.pallas_call(
        cut_kernel,
        grid_spec=pltpu.PrefetchScalarGridSpec(
            num_scalar_prefetch=1,
            grid=(1,),
            in_specs=[pl.BlockSpec((high, total), lambda i, where: (where[1], 0))],
            out_specs=[pl.BlockSpec((high, depth), lambda i, where: (0, 0))] * count,
            scratch_shapes=[pltpu.VMEM((count, high, depth), jnp.bfloat16)],
        ),
        out_shape=[jax.ShapeDtypeStruct((high, depth), jnp.bfloat16)] * count,
        compiler_params=params("arbitrary", limit=CUT_LIMIT),
        cost_estimate=SMALL,
        name="cut_blocks",
    )(jnp.stack([pair, part, core]), in_hbm(amplitudes))


def pack_kernel(count, *refs):
    for n in range(count):
        refs[-1][n] = refs[n][...]


def pack(blocks, others):
    shape = (len(blocks),) + blocks[0].shape
    return pl.pallas_call(
        functools.partial(pack_kernel, len(blocks)),
        in_specs=[pl.BlockSpec(memory_space=pltpu.VMEM)] * len(blocks)
        + [pl.BlockSpec(memory_space=pl.ANY)] * len(others),
        out_shape=jax.ShapeDtypeStruct(shape, jnp.bfloat16),
        compiler_params=params(limit=CUT_LIMIT),
        cost_estimate=SMALL,
        name="pack_blocks",
    )(*blocks, *others)


def product_kernel(order, parts, cols, segments, where, *refs):
    a_refs, (h_ref, v_ref, o_ref), outs = refs[:parts], refs[parts : parts + 3], refs[parts + 3 : -4]
    left, left_rest, right_rest, codes = refs[-4:]
    part, depth = a_refs[0].shape[1] // parts, a_refs[0].shape[2]
    rows = o_ref.shape[0]
    main, second = split_depth(depth)
    step = pl.program_id(0)
    tile = v_ref.shape[1]
    high = outs[0].shape[0]

    @pl.when(step == 0)
    def _():
        left_rest[...] = jnp.zeros_like(left_rest)
        right_rest[...] = jnp.zeros_like(right_rest)
        count = a_refs[0].shape[0]
        spot = {entry: n for n, entry in enumerate(order)}
        for s, ref in enumerate(a_refs):
            swapped = where[1] ^ s
            for j in range(count):
                low = (j + 1) % count
                for q in range(parts):
                    near, far = spot[q, low], spot[q, low + count]
                    at = jnp.where(swapped == 0, near, far) * part
                    at = pl.ds(pl.multiple_of(at, part), part)
                    block = ref.at[j, q * part : (q + 1) * part]
                    left[at, :] = block[:, :main]
                    left_rest[at, : depth - main] = block[:, main:]
                    source = where[0] ^ (low + count * swapped)
                    left_rest[at, second : second + rows] = h_ref[source, where[2 + q]]

    right_rest[: depth - main, :] = v_ref[main:, :]
    right_rest[second : second + rows, :] = o_ref[...]
    acc = jnp.dot(left[...], v_ref[:main, :], preferred_element_type=jnp.float32)
    acc = acc + jnp.dot(left_rest[...], right_rest[...], preferred_element_type=jnp.float32)
    acc = jnp.where(columns(acc.shape[0], tile, step * tile) < cols, acc, 0.0)
    given = parts * high
    for j in range(parts):
        outs[parts + j][...] = acc[given + j * high : given + (j + 1) * high]
    whole, code = encode(acc[:given])
    at = lax.broadcasted_iota(jnp.int32, codes.shape, 1)
    codes[...] = jnp.where(at == step, code, codes[...])

    @pl.when(step < segments - 1)
    def _():
        for j in range(parts):
            outs[j][...] = whole[j * high : (j + 1) * high].astype(jnp.int16)

    @pl.when(step == segments - 1)
    def _():
        kept = [codes[:, n : n + 1] for n in range(segments)]
        done = with_codes(whole, kept, cols, (segments - 1) * tile)
        for j in range(parts):
            outs[j][...] = done[j * high : (j + 1) * high].astype(jnp.int16)


def split_depth(depth):
    main = depth // LANES * LANES
    return main, -(-(depth - main) // 16) * 16


def product(order, where, sources, holes, integrals, own_cols, give_space):
    parts = len(sources)
    _, high_block, depth = sources[0].shape
    part = high_block // parts
    cols = integrals.shape[1]
    rows = own_cols.shape[0]
    width, segments = layout(cols)
    tile = width // segments
    total = len(order) * part
    high = total // (2 * parts)
    main, second = split_depth(depth)
    rest = -(-(second + rows) // LANES) * LANES
    whole = lambda x: pl.BlockSpec(x.shape, lambda i, where: (0,) * x.ndim)
    out = pl.BlockSpec((high, tile), lambda i, where: (0, i))
    return pl.pallas_call(
        functools.partial(product_kernel, order, parts, cols, segments),
        grid_spec=pltpu.PrefetchScalarGridSpec(
            num_scalar_prefetch=1,
            grid=(segments,),
            in_specs=[whole(x) for x in sources]
            + [
                whole(holes),
                pl.BlockSpec((depth, tile), lambda i, where: (0, i)),
                pl.BlockSpec((rows, tile), lambda i, where: (0, i)),
            ],
            out_specs=[out] * (2 * parts),
            scratch_shapes=[
                pltpu.VMEM((total, main), jnp.bfloat16),
                pltpu.VMEM((total, rest), jnp.bfloat16),
                pltpu.VMEM((rest, tile), jnp.bfloat16),
                pltpu.VMEM((total // 2, LANES), jnp.float32),
            ],
        ),
        out_shape=[give_space((high, width), jnp.int16)] * parts
        + [jax.ShapeDtypeStruct((high, width), jnp.float32)] * parts,
        compiler_params=params("arbitrary"),
        cost_estimate=SMALL,
        name="partial_products",
    )(where, *sources, in_hbm(holes), integrals, in_hbm(own_cols))


def add_kernel(cols, segments, inputs, inner, *refs):
    keeps, coded, (give_ref, next_ref) = refs[:inputs], refs[inputs : 2 * inputs], refs[2 * inputs :]
    high, width = next_ref.shape
    half = high // (inputs * inner)
    tile = width // segments
    chunk = min(16, half)

    for index in range(inputs):
        keep_ref, coded_ref = keeps[index], coded[index]

        def total(at, n, codes):
            span = slice(n * tile, (n + 1) * tile)
            return keep_ref[at, span] + decode(coded_ref[at, span], codes, n, cols, n * tile)

        for group in range(inner):
            top, target = 2 * half * group, half * (inner * index + group)

            @pl.loop(0, half // chunk)
            def _(i):
                out = pl.ds(pl.multiple_of(target + i * chunk, chunk), chunk)
                at = pl.ds(pl.multiple_of(top + i * chunk, chunk), chunk)
                codes = codes_of(coded_ref, at, cols, segments)
                made = []
                for n in range(segments):
                    whole, code = encode(total(at, n, codes))
                    made.append(code)
                    if n == segments - 1:
                        whole = with_codes(whole, made, cols, n * tile)
                    give_ref[out, n * tile : (n + 1) * tile] = whole.astype(jnp.int16)

            @pl.loop(0, half // chunk)
            def _(i):
                out = pl.ds(pl.multiple_of(target + i * chunk, chunk), chunk)
                at = pl.ds(pl.multiple_of(top + half + i * chunk, chunk), chunk)
                codes = codes_of(coded_ref, at, cols, segments)
                for n in range(segments):
                    next_ref[out, n * tile : (n + 1) * tile] = total(at, n, codes)


def add(keeps, coded, inner, cols):
    high, width = keeps[0].shape
    out = (len(keeps) * high // 2, width)
    return pl.pallas_call(
        functools.partial(add_kernel, cols, layout(cols)[1], len(keeps), inner),
        out_shape=(
            jax.ShapeDtypeStruct(out, jnp.int16),
            jax.ShapeDtypeStruct(out, jnp.float32),
        ),
        compiler_params=params(),
        cost_estimate=SMALL,
        name="add_partial_sums",
    )(*keeps, *coded)


def update_kernel(cols, segments, inputs, where, *refs):
    keeps, coded, (d_ref, v_ref, o_ref, out_ref) = refs[:inputs], refs[inputs : 2 * inputs], refs[2 * inputs :]
    width = out_ref.shape[1]
    tile = width // segments
    part = out_ref.shape[0] // 2
    for j in range(2):
        keep_ref, coded_ref = keeps[j % inputs], coded[j % inputs]
        at = pl.ds((j // inputs) * part, part)
        here = pl.ds(pl.multiple_of(where[j] * part, part), part)
        mine = pl.ds(pl.multiple_of((where[j] % 2) * part, part), part)
        codes = codes_of(coded_ref, at, cols, segments)
        made = []
        for n in range(segments):
            start, stop = n * tile, (n + 1) * tile
            ladder = keep_ref[at, start:stop]
            ladder = ladder + decode(coded_ref[at, start:stop], codes, n, cols, start)
            driver = d_ref[mine, start : min(stop, cols)].astype(jnp.float32)
            if stop > cols:
                driver = jnp.concatenate(
                    [driver, jnp.zeros((part, stop - cols), jnp.float32)], axis=1
                )
            gap = v_ref[:, start:stop] - o_ref[here, 0:1]
            whole, code = encode((driver + ladder) / gap)
            made.append(code)
            if n == segments - 1:
                whole = with_codes(whole, made, cols, start)
            out_ref[j * part : (j + 1) * part, start:stop] = whole.astype(jnp.int16)


def updated(keeps, coded, driver, pair_energy, hole_energy, where, cols):
    high, width = keeps[0].shape
    high *= len(keeps)
    whole = lambda x: pl.BlockSpec(x.shape, lambda i, where: (0,) * x.ndim)
    return pl.pallas_call(
        functools.partial(update_kernel, cols, layout(cols)[1], len(keeps)),
        grid_spec=pltpu.PrefetchScalarGridSpec(
            num_scalar_prefetch=1,
            grid=(1,),
            in_specs=[whole(x) for x in (*keeps, *coded)]
            + [pl.BlockSpec((high, cols), lambda i, where: (where[0] // 2, 0))]
            + [whole(pair_energy), whole(hole_energy)],
            out_specs=pl.BlockSpec((high, width), lambda i, where: (0, 0)),
        ),
        out_shape=jax.ShapeDtypeStruct((high, width), jnp.int16),
        compiler_params=params("arbitrary"),
        cost_estimate=SMALL,
        name="update_amplitudes",
    )(where, *keeps, *coded, driver, pair_energy, hole_energy)


def place_kernel(cols, segments, groups, where, *refs):
    out_ref, slots = refs[-2:]
    rows = out_ref.shape[0]
    part = rows // 4
    width = refs[0].shape[1]
    tile = width // segments
    for index in range(2 * groups):
        rel, half = index // 2, index % 2
        ref = refs[index]
        group = where[0] ^ rel
        shift = (group * cols) % LANES
        for j in range(2):
            at = pl.ds(j * part, part)
            codes = codes_of(ref, at, cols, segments)
            pieces = [
                decode(ref[at, n * tile : (n + 1) * tile], codes, n, cols, n * tile)
                for n in range(segments)
            ]
            pieces += [jnp.zeros((part, slots.shape[2] - width), jnp.float32)] * (
                slots.shape[2] > width
            )
            x = pltpu.roll(jnp.concatenate(pieces, axis=1), shift, 1)
            quarter = 2 * ((group // 2) % 2 ^ half) + j
            slots[group, pl.ds(pl.multiple_of(quarter * part, part), part), :] = x
    lane = lax.broadcasted_iota(jnp.int32, (rows, LANES), 1)
    for group in range(groups):
        start = group * cols
        base, shift = start // LANES * LANES, start % LANES
        full = (shift + cols) // LANES * LANES
        if group == groups - 1:
            full = shift + cols
        first = 0
        if shift:
            before = (group - 1) * cols % LANES + cols
            before = before // LANES * LANES
            tail = slots[group - 1, :, before : before + LANES]
            out_ref[:, base : base + LANES] = jnp.where(
                lane < shift, tail, slots[group, :, 0:LANES]
            )
            first = LANES
        out_ref[:, base + first : base + full] = slots[group, :, first:full]


def place(blocks, grp, rows, cols, groups):
    width, segments = layout(cols)
    unit = math.gcd(cols, LANES)
    room = width + LANES * (cols % LANES > unit)
    whole = lambda shape: pl.BlockSpec(shape, lambda i, where: (0,) * len(shape))
    out = (rows, groups * cols)
    return pl.pallas_call(
        functools.partial(place_kernel, cols, segments, groups),
        grid_spec=pltpu.PrefetchScalarGridSpec(
            num_scalar_prefetch=1,
            grid=(1,),
            in_specs=[whole(x.shape) for x in blocks],
            out_specs=whole(out),
            scratch_shapes=[pltpu.VMEM((groups, rows, room), jnp.float32)],
        ),
        out_shape=jax.ShapeDtypeStruct(out, jnp.float32),
        compiler_params=params("arbitrary"),
        name="place_columns",
    )(grp, *blocks)


def spans_of(cols, chip):
    first = chip * 2 * cols % LANES
    second = first + cols
    return first, second // LANES, second % LANES, -(-(second + cols) // LANES)


def half_kernel(cols, segments, late, where, *refs):
    coded, refs = refs[:4], refs[4:]
    if late:
        seam_in, _, out_ref, strips, sems = refs
    else:
        out_ref, seam_ref, strips, sems = refs
    high = coded[0].shape[0]
    part = high // 2
    width = coded[0].shape[1]
    tile = width // segments
    for chip in range(2):
        seam = spans_of(cols, chip)[1] * LANES
        strips[chip, :, seam : seam + LANES] = jnp.zeros((high, LANES), jnp.float32)
    for rel, ref in enumerate(coded):
        for group in range(4):

            @pl.when(where[0] ^ rel == group)
            def _():
                shift = group * cols % LANES
                strip = strips.at[group // 2]
                seam = spans_of(cols, group // 2)[1] * LANES
                for j in range(2):
                    at = slice(j * part, (j + 1) * part)
                    codes = codes_of(ref, at, cols, segments)
                    pieces = [
                        decode(ref[at, n * tile : (n + 1) * tile], codes, n, cols, n * tile)
                        for n in range(segments)
                    ]
                    x = jnp.concatenate(pieces, axis=1)
                    x = pltpu.roll(x, shift, 1) if shift else x
                    if group % 2:
                        tiles = spans_of(cols, group // 2)[3]
                        strip[at, seam + LANES : tiles * LANES] = x[:, LANES : tiles * LANES - seam]
                        strip[at, seam : seam + LANES] += x[:, :LANES]
                    else:
                        strip[at, :seam] = x[:, :seam]
                        strip[at, seam : seam + LANES] += x[:, seam : seam + LANES]
    stores = []
    for chip in range(2):
        tiles = spans_of(cols, chip)[3]
        strip = strips.at[chip]
        top = (chip ^ late) * high
        shared = slice(0, LANES) if chip else slice((tiles - 1) * LANES, tiles * LANES)
        if late:
            strip[:, shared] = strip[:, shared] + seam_in[top : top + high, :]
            start, stop = 0, tiles * LANES
        else:
            seam_ref[top : top + high, :] = strip[:, shared]
            start, stop = (LANES, tiles * LANES) if chip else (0, (tiles - 1) * LANES)
        base = chip * 2 * cols // LANES * LANES
        store = pltpu.make_async_copy(
            strip.at[:, start:stop],
            out_ref.at[top : top + high, base + start : base + stop],
            sems.at[chip],
        )
        store.start()
        stores.append(store)
    for store in stores:
        store.wait()


def place_half(blocks, grp, rows, cols, so_far=None):
    width, segments = layout(cols)
    high = rows // 2
    tiles = max(spans_of(cols, chip)[3] for chip in range(2))
    whole = lambda x: pl.BlockSpec(x.shape, lambda i, where: (0,) * x.ndim)
    anywhere = pl.BlockSpec(memory_space=pl.ANY)
    out = jax.ShapeDtypeStruct((rows, 4 * cols), jnp.float32)
    seam = jax.ShapeDtypeStruct((rows, LANES), jnp.float32)
    late = so_far is not None
    return pl.pallas_call(
        functools.partial(half_kernel, cols, segments, late),
        grid_spec=pltpu.PrefetchScalarGridSpec(
            num_scalar_prefetch=1,
            grid=(1,),
            in_specs=[whole(x) for x in blocks] + [whole(seam), anywhere] * late,
            out_specs=anywhere if late else (anywhere, whole(seam)),
            scratch_shapes=[
                pltpu.VMEM((2, high, tiles * LANES), jnp.float32),
                pltpu.SemaphoreType.DMA((2,)),
            ],
        ),
        out_shape=out if late else (out, seam),
        input_output_aliases={6: 0} if late else {},
        compiler_params=params("arbitrary"),
        name="place_late_half" if late else "place_early_half",
    )(grp, *blocks, *(so_far[::-1] if late else ()))


def shards(amplitudes, integrals, hole_ints, driver, e_occ, e_virt, occ_pairs, virt_pairs):
    groups, pairs = lax.axis_size("grp"), lax.axis_size("pair")
    grp, pair = lax.axis_index("grp"), lax.axis_index("pair")
    rows = amplitudes.shape[0]
    part = rows // 4
    depth, cols = integrals.shape
    width, _ = layout(cols)

    def swap(x, axis, flip):
        size = lax.axis_size(axis)
        return lax.ppermute(x, axis, [(i, i ^ flip) for i in range(size)])

    own_cols = lax.dynamic_slice_in_dim(amplitudes, grp * cols, cols, 1)
    holes = lax.dynamic_slice_in_dim(hole_ints, pair * rows, rows, 1)
    holes = holes.reshape(pairs, 4, part, rows)
    occ_energy = lookup(occ_pairs, e_occ)
    virt_energy = lookup(virt_pairs, e_virt)
    hole_energy = jnp.broadcast_to((occ_energy[0] + occ_energy[1])[:, None], (rows, LANES))
    pair_energy = jnp.pad(
        (virt_energy[0] + virt_energy[1])[None, :],
        ((0, 0), (0, width - cols)),
        constant_values=8.0,
    )

    chip_half, core_at, count = (grp // 2) % 2, grp % 2, pairs // 2
    blocks = list(cut(amplitudes, pair, chip_half, core_at, pairs, depth))
    for j in range(count):
        moves = [
            (g * pairs + p, g * pairs + (p ^ (g % 2 * count + (j + 1) % count)))
            for g in range(groups)
            for p in range(pairs)
        ]
        blocks[j] = lax.ppermute(blocks[j], ("grp", "pair"), moves)
    own = pack(blocks, (own_cols, holes, pair_energy, hole_energy))
    core = pack([swap(x, "grp", 1) for x in blocks], ())
    chip = swap(own, "grp", 2)

    bits = [1 << n for n in range(pairs.bit_length() - 1)]
    x_first, z_first = bits, bits[1::-1] + bits[2:]
    x_then_far = bits[:1] + bits[2:] + bits[1:2]
    routes = ((z_first, x_then_far), (x_first, z_first))

    def listed(value, left):
        if not left:
            return [value]
        return listed(value | left[0], left[1:]) + listed(value, left[1:])

    def place_of(half):
        first = 2 * (chip_half ^ half)
        return jnp.stack([first, first + 1])

    def products(half, *sources):
        given = [(q, k) for q, r in enumerate(routes[half]) for k in listed(r[0], r[1:])]
        order = given + [(q, k ^ routes[half][q][0]) for q, k in given]
        where = jnp.concatenate([jnp.stack([pair, core_at]), place_of(half)])
        space = jax.ShapeDtypeStruct if half else pltpu.HBM
        made = product(order, where, sources, holes, integrals, own_cols, space)
        return list(zip(made[:2], made[2:]))

    first = products(0, own, core)
    chip, _ = lax.optimization_barrier((chip, first[0][1]))
    both = swap(chip, "grp", 1)
    second = products(1, chip, both)

    state = [first, second]
    for n in range(len(bits)):
        for half in range(2):
            one, two = routes[half]
            steps = [one[n]] if len(state[half]) == 1 else [one[n], two[n]]
            got = [swap(give, "pair", bit) for (give, _), bit in zip(state[half], steps)]
            keeps = [keep for _, keep in state[half]]
            inner = 3 - len(keeps)
            if n == len(bits) - 1:
                state[half] = (keeps, got)
            elif inner == 2:
                state[half] = [add(keeps, got, inner, cols)]
            else:
                state[half] = [add([k], [g], 1, cols) for k, g in zip(keeps, got)]
    sent = []
    in_halves = groups == 4 and 2 * cols % LANES != 0
    for half in range(2):
        keeps, got = state[half]
        coded = updated(keeps, got, driver, pair_energy, hole_energy, place_of(half), cols)
        here = [coded] + [swap(coded, "grp", 2 * k) for k in range(1, groups // 2)]
        if half and in_halves:
            early = place_half(sent[0], grp[None], rows, cols)
        sent.append([x for own_x in here for x in (own_x, swap(own_x, "grp", 1))])

    if in_halves:
        return place_half(sent[1], grp[None], rows, cols, early)
    ordered = [sent[half][rel] for rel in range(groups) for half in range(2)]
    return place(ordered, grp[None], rows, cols, groups)


def solution(mesh):
    placed = (
        P("pair", None),
        P("pair", "grp"),
        P(),
        P("pair", "grp"),
        P(),
        P(),
        P(None, "pair"),
        P(None, "grp"),
    )
    return jax.shard_map(
        shards, mesh=mesh, in_specs=placed, out_specs=P("pair", None), check_vma=False
    )
```
